32 devices in a mesh: groups: 2 (over y), blk: 8 (over z, x), head: 2 (over core).
Axes of the slice: x: 2, y: 2, z: 4, core: 2. Of those that a mesh axis runs over, the one named last changes fastest.
Arguments:
- tokens: float32 [3072, 1024], P(('groups', 'blk'), 'head'), parts along dimension 0, may hold values from -20 to 20
- norm_gain: float32 [1024], replicated, may hold values from 0.1 to 1.9
- qkv_weight: bfloat16 [3, 1024, 1024], P(None, None, 'head'), may hold values from -20 to 20
- out_weight: bfloat16 [1024, 1024], P('head'), may hold values from -0.1875 to 0.1875
- lateral_weight: bfloat16 [2, 1024, 256], replicated, may hold values from -0.1875 to 0.1875
- conv_weight: bfloat16 [2, 3, 3, 256, 256], replicated, may hold values from -0.125 to 0.125
- level_gains: float32 [2, 2, 256], replicated, may hold values from 0.1 to 1.9
Outputs:
- fine_map: bfloat16 [32, 96, 256], P(('groups', 'blk'), 'head'), parts along dimension 0
- coarse_map: bfloat16 [16, 48, 256], P(('groups', 'blk'), 'head'), parts along dimension 0
The draws below stay inside these ranges and needn't reach their ends.
There are 2 independent parts, one for each index of `groups`. The reference program is written for one: setup_inputs(seed, part) draws one part's arguments, and reference() takes and returns one part's arrays. A program takes and returns all parts, laid end to end along the dimension named above; an argument that names none is the same for every part. Nothing has to cross between parts.
All inputs are finite; a program needn't handle non-finite values.
Results may differ from the reference program's by a relative error of at most 0.014.
The reference program's roundings to bfloat16 on the way count: a program that leaves them out, or rounds other values in their place, can miss the bound.
Values may be sent and summed in bfloat16 or wider, within the bound.
A program may use at most 128 MiB of HBM per device.

```python
import math
import jax
import jax.numpy as jnp
from jax import lax

D = 1024
HEADS = 16
HEAD_DIM = 64
CHANNELS = 256
GW = 96
GH = 16
TOKENS = 1536


def draw_tokens(key, part):
    normal_base = jnp.clip(jax.random.normal(jax.random.fold_in(key, 11), (TOKENS, D), jnp.float32), -6.0, 6.0)
    return 0.4 * normal_base


def draw_qkv_weight(key, part):
    normal_base = jnp.clip(jax.random.normal(jax.random.fold_in(key, 21), (3, D, D), jnp.float32), -6.0, 6.0)
    std_match = 1.58 / math.sqrt(D)
    std_value = 2.0 / math.sqrt(D)
    scales = jnp.array([std_match, std_match, std_value], jnp.float32)[:, None, None]
    weights = normal_base * scales
    return weights.astype(jnp.bfloat16)


def block_scale(stream_key, shape, pieces, smallest, high):
    loudness, own = 1.0, jax.random.fold_in(stream_key, 6)
    for position, shards_of in pieces:
        heights = jnp.exp(jax.random.uniform(jax.random.fold_in(own, position), (shards_of,), jnp.float32, smallest / len(pieces), high / len(pieces)))
        loudness = loudness * jnp.repeat(heights, shape[position] // shards_of).reshape([-1 if axis == position else 1 for axis in range(len(shape))])
    return loudness


def noise(rng, dims, deviation, limit, pieces=(), kind=jnp.bfloat16):
    gain = block_scale(rng, dims, pieces, -0.22, 0.18) if pieces else 1.0
    drawn = jax.random.normal(rng, dims, jnp.float32) * deviation * gain
    return jnp.minimum(jnp.maximum(drawn, -limit), limit).astype(kind)


def setup_inputs(seed: int = 0, part: int = 0) -> dict:
    splits = jax.random.split(jax.random.key(seed), 8)
    part_splits = jax.random.split(jax.random.fold_in(splits[7], part), 8)
    return {
        "tokens": draw_tokens(jax.random.fold_in(jax.random.fold_in(splits[7], part), 71), part),
        "norm_gain": jnp.clip(1.0 + 0.18 * jax.random.normal(splits[1], (D,), jnp.float32), 0.1, 1.9),
        "qkv_weight": draw_qkv_weight(jax.random.fold_in(splits[7], 71), part),
        "out_weight": noise(splits[3], (D, D), D ** -0.5, 0.1875, ((0, 2),)),
        "lateral_weight": noise(splits[4], (2, D, CHANNELS), D ** -0.5, 0.1875),
        "conv_weight": noise(splits[5], (2, 3, 3, CHANNELS, CHANNELS), (9 * CHANNELS) ** -0.5, 0.125),
        "level_gains": jnp.clip(1.0 + 0.18 * jax.random.normal(splits[6], (2, 2, CHANNELS), jnp.float32), 0.1, 1.9),
    }


def layer_norm(values_in, gain_row):
    mean_row = lax.optimization_barrier(jnp.mean(values_in, axis=-1, keepdims=True))
    centred = values_in - mean_row
    spread = lax.optimization_barrier(jnp.mean(centred * centred, axis=-1, keepdims=True))
    return centred * lax.rsqrt(spread + 1e-06) * gain_row

def attention(queries, key_rows, value_rows):
    token_count = queries.shape[0]
    query_rows = math.gcd(token_count, 2048)
    block_count = token_count // query_rows
    score_scale = HEAD_DIM ** (-0.5)

    def single_head(head_index):
        query_head = lax.dynamic_slice_in_dim(queries, head_index * HEAD_DIM, HEAD_DIM, 1)
        key_head = lax.dynamic_slice_in_dim(key_rows, head_index * HEAD_DIM, HEAD_DIM, 1)
        value_head = lax.dynamic_slice_in_dim(value_rows, head_index * HEAD_DIM, HEAD_DIM, 1)

        def single_block(block_index):
            query_block = lax.dynamic_slice_in_dim(query_head, block_index * query_rows, query_rows, 0)
            scores = jnp.dot(query_block, key_head.T, preferred_element_type=jnp.float32) * score_scale
            weights = jnp.exp(scores - lax.optimization_barrier(jnp.max(scores, axis=-1, keepdims=True)))
            totals = lax.optimization_barrier(jnp.sum(weights, axis=-1, keepdims=True))
            mixed = jnp.dot(weights.astype(jnp.bfloat16), value_head, preferred_element_type=jnp.float32)
            return (mixed / totals).astype(jnp.bfloat16)
        blocks = lax.map(single_block, jnp.arange(block_count, dtype=jnp.int32))
        return blocks.reshape(token_count, HEAD_DIM)
    per_head = lax.map(single_head, jnp.arange(HEADS, dtype=jnp.int32))
    return jnp.transpose(per_head, (1, 0, 2)).reshape(token_count, HEADS * HEAD_DIM)

def pyramid_level(grid_in, lateral, kernel, gains):
    mixed = jnp.einsum('rcd,de->rce', grid_in.astype(jnp.float32), lateral.astype(jnp.float32))
    lateral_out = layer_norm(mixed, gains[0]).astype(jnp.bfloat16)
    row_count = grid_in.shape[0]
    col_count = grid_in.shape[1]
    padded = jnp.pad(lateral_out, ((1, 1), (1, 1), (0, 0)))
    total_out = jnp.zeros((row_count, col_count, kernel.shape[-1]), jnp.float32)
    for tap_row in range(3):
        for tap_col in range(3):
            window = padded[tap_row:tap_row + row_count, tap_col:tap_col + col_count]
            total_out = total_out + jnp.einsum('rcd,de->rce', window.astype(jnp.float32), kernel[tap_row, tap_col].astype(jnp.float32))
    return layer_norm(total_out, gains[1]).astype(jnp.bfloat16)

def reference(tokens, norm_gain, qkv_weight, out_weight, lateral_weight, conv_weight, level_gains):
    normed = layer_norm(tokens, norm_gain).astype(jnp.bfloat16)
    queries = jnp.dot(normed, qkv_weight[0], preferred_element_type=jnp.float32).astype(jnp.bfloat16)
    key_rows = jnp.dot(normed, qkv_weight[1], preferred_element_type=jnp.float32).astype(jnp.bfloat16)
    value_rows = jnp.dot(normed, qkv_weight[2], preferred_element_type=jnp.float32).astype(jnp.bfloat16)
    attended = attention(queries, key_rows, value_rows)
    block_out = (tokens + jnp.dot(attended, out_weight, preferred_element_type=jnp.float32)).astype(jnp.bfloat16)
    grid = block_out.reshape(GH, GW, D)
    pooled = lax.optimization_barrier(jnp.max(grid.reshape(GH // 2, 2, GW // 2, 2, D), axis=(1, 3)))
    fine_map = pyramid_level(grid, lateral_weight[0], conv_weight[0], level_gains[0])
    coarse_map = pyramid_level(pooled, lateral_weight[1], conv_weight[1], level_gains[1])
    return (fine_map, coarse_map)
```

```python
import functools

import jax
import jax.numpy as jnp
from jax import lax
from jax.experimental import pallas as pl
from jax.experimental.pallas import tpu as pltpu
from jax.sharding import PartitionSpec as P

HEAD_DIM = 64
ROWS_DEV = 2
GW = 96
SUBS = 2
F32 = jnp.float32
BF16 = jnp.bfloat16
NT = (((1,), (1,)), ((), ()))


def layer_norm(values_in, gain_row):
    mean_row = jnp.mean(values_in, axis=-1, keepdims=True)
    centred = values_in - mean_row
    spread = jnp.mean(centred * centred, axis=-1, keepdims=True)
    return centred * lax.rsqrt(spread + 1e-06) * gain_row


def dot(lhs, rhs):
    return jnp.dot(lhs, rhs, preferred_element_type=F32)


def dot_nt(lhs, rhs):
    return lax.dot_general(lhs, rhs, NT, preferred_element_type=F32)


def kernel(
    count,
    tokens_ref, gain_ref, qkv_hbm, out_hbm, lateral_hbm, conv_hbm, gains_ref,
    fine_ref, coarse_ref,
    tok, qkv, out_w, lat_w, conv_w, wvt, normed, ring, other, qbd, kbuf, vbuf,
    acc, peak, total, att, part_send, part_recv, fpad, cpad, fcol, ccol,
    load_sem, tok_sem, ring_send, ring_recv, sib_send, sib_recv, part_sem, halo_send, halo_recv,
):
    blk = lax.axis_index("blk")
    head = lax.axis_index("head")
    sib = 1 - head
    rows = tok.shape[1]
    half = rows // 2
    cols = GW // 2
    pairs = qbd.shape[0]
    pair_rows = qbd.shape[1]

    even = blk % 2 == 0
    up_ring = jnp.where(
        even, jnp.where(blk == count - 2, blk + 1, blk + 2), jnp.where(blk == 1, blk - 1, blk - 2)
    )
    down_ring = jnp.where(
        even, jnp.where(blk == 0, blk + 1, blk - 2), jnp.where(blk == count - 1, blk - 1, blk + 2)
    )
    target = jnp.where(head == 0, up_ring, down_ring)
    source = jnp.where(head == 0, down_ring, up_ring)

    loads = [
        pltpu.make_async_copy(tokens_ref, tok.at[head], load_sem.at[0]),
        pltpu.make_async_copy(qkv_hbm.at[2], qkv.at[2], load_sem.at[1]),
        pltpu.make_async_copy(qkv_hbm.at[0], qkv.at[0], load_sem.at[2]),
        pltpu.make_async_copy(qkv_hbm.at[1], qkv.at[1], load_sem.at[3]),
        pltpu.make_async_copy(out_hbm, out_w, load_sem.at[4]),
        pltpu.make_async_copy(lateral_hbm, lat_w, load_sem.at[5]),
        pltpu.make_async_copy(conv_hbm, conv_w, load_sem.at[6]),
    ]
    for load in loads:
        load.start()

    fpad[...] = jnp.zeros_like(fpad)
    cpad[...] = jnp.zeros_like(cpad)

    barrier = pltpu.get_barrier_semaphore()

    def greet(to_blk, to_head):
        pl.semaphore_signal(barrier, inc=1, device_id={"blk": to_blk, "head": to_head})

    greet(blk, sib)
    greet(target, head)
    greet(source, head)

    has_up = blk > 0
    has_down = blk < count - 1

    @pl.when(has_up)
    def _():
        greet(blk - 1, head)
        greet(blk - 1, sib)

    @pl.when(has_down)
    def _():
        greet(blk + 1, head)
        greet(blk + 1, sib)

    pl.semaphore_wait(barrier, 3 + 2 * has_up.astype(jnp.int32) + 2 * has_down.astype(jnp.int32))

    def remote(src, dst, send, recv, to_blk, to_head):
        return pltpu.make_async_remote_copy(
            src_ref=src, dst_ref=dst, send_sem=send, recv_sem=recv,
            device_id={"blk": to_blk, "head": to_head},
        )

    tok_copy = remote(tokens_ref, tok.at[head], tok_sem.at[0], tok_sem.at[1], blk, sib)
    tok_copy.start()

    acc[...] = jnp.zeros_like(acc)
    total[...] = jnp.zeros_like(total)
    peak[...] = jnp.full(peak.shape, -jnp.inf, F32)

    def ring_copy(step, sub):
        return remote(
            ring.at[step, sub], ring.at[step + 1, sub],
            ring_send.at[step, sub], ring_recv.at[step + 1, sub], target, head,
        )

    def sib_copy(step, sub):
        return remote(
            ring.at[step, sub], other.at[step, sub],
            sib_send.at[step, sub], sib_recv.at[step, sub], blk, sib,
        )

    loads[0].wait()
    tok_copy.wait()
    left, right = tok[0], tok[1]
    width = left.shape[1] + right.shape[1]
    mean_row = (
        jnp.sum(left, axis=-1, keepdims=True) + jnp.sum(right, axis=-1, keepdims=True)
    ) / width
    left = left - mean_row
    right = right - mean_row
    spread = (
        jnp.sum(left * left, axis=-1, keepdims=True) + jnp.sum(right * right, axis=-1, keepdims=True)
    ) / width
    scale = lax.rsqrt(spread + 1e-06)
    gain = gain_ref[...]
    wide = left.shape[1]
    normed[:, :wide] = (left * scale * gain[:, :wide]).astype(BF16)
    normed[:, wide:] = (right * scale * gain[:, wide:]).astype(BF16)
    piece = half // SUBS
    for sub in range(SUBS):
        ring[0, sub] = normed[pl.ds(pl.multiple_of(head * half + sub * piece, 16), piece), :]
    for sub in range(SUBS):
        ring_copy(0, sub).start()
    for sub in range(SUBS):
        other[0, sub] = normed[pl.ds(pl.multiple_of(sib * half + sub * piece, 16), piece), :]

    loads[1].wait()
    wvt[...] = qkv[2].T
    loads[2].wait()
    queries = (dot(normed[...], qkv[0]) * (HEAD_DIM ** -0.5)).astype(BF16)
    per_pair = 2 * HEAD_DIM
    quad = qbd.shape[2]
    lane = lax.broadcasted_iota(jnp.int32, (rows, quad), 1)
    for pair in range(pairs):
        base = pair * per_pair // quad * quad
        block = queries[:, base : base + quad]
        for inner in range(2):
            first = pair * per_pair + inner * HEAD_DIM - base
            keep = (lane >= first) & (lane < first + HEAD_DIM)
            qbd[pair, inner * rows : (inner + 1) * rows, :] = jnp.where(keep, block, jnp.zeros_like(block))
    loads[3].wait()

    def project(step):
        chunk = jnp.concatenate(
            [ring[step].reshape(half, width), other[step].reshape(half, width)], axis=0
        )
        kbuf[...] = dot(chunk, qkv[1]).astype(BF16)
        vbuf[...] = dot_nt(wvt[...], chunk).astype(BF16)

    def attend():
        for pair in range(pairs):
            base = pair * per_pair // quad * quad
            scores = dot_nt(kbuf[:, base : base + quad], qbd[pair])
            before = peak[pair]
            now = jnp.maximum(before, jnp.max(scores, axis=0, keepdims=True))
            weights = jnp.exp(scores - now)
            factor = jnp.exp(before - now)
            peak[pair] = now
            total[pair] = total[pair] * factor + jnp.sum(weights, axis=0, keepdims=True)
            mixed = dot(vbuf[pair * per_pair : (pair + 1) * per_pair, :], weights.astype(BF16))
            acc[pair] = acc[pair] * factor + mixed

    def ring_step(step, carry):
        for sub in range(SUBS):
            ring_copy(step - 1, sub).wait_recv()

            @pl.when(step < count - 1)
            def _():
                ring_copy(step, sub).start()

            sib_copy(step, sub).start()
            if sub == 0:
                @pl.when(step > 1)
                def _():
                    for piece_sub in range(SUBS):
                        sib_copy(step - 1, piece_sub).wait_recv()

                project(step - 1)
            if sub == SUBS - 1:
                attend()
        return carry

    lax.fori_loop(1, count, ring_step, 0)
    for sub in range(SUBS):
        sib_copy(count - 1, sub).wait_recv()
    project(count - 1)
    attend()

    pair_lane = lax.broadcasted_iota(jnp.int32, (rows, per_pair), 1)
    for pair in range(pairs):
        done = (acc[pair] / total[pair]).T
        att[:, pair * per_pair : (pair + 1) * per_pair] = jnp.where(
            pair_lane < HEAD_DIM, done[:rows], done[rows:]
        ).astype(BF16)

    loads[4].wait()

    def tile_rows(ref, side):
        return jnp.concatenate(
            [
                ref[pl.ds(pl.multiple_of(side * cols + row * GW, 16), cols), :]
                for row in range(ROWS_DEV)
            ],
            axis=0,
        )

    part_send[...] = dot(tile_rows(att, sib), out_w[...]).astype(BF16)
    part_copy = remote(part_send, part_recv, part_sem.at[0], part_sem.at[1], blk, sib)
    part_copy.start()
    own = dot(tile_rows(att, head), out_w[...])
    residual = jnp.concatenate([tile_rows(tok.at[0], head), tile_rows(tok.at[1], head)], axis=1)
    own = own + residual
    loads[5].wait()
    loads[6].wait()
    part_copy.wait()
    block_out = (own + part_recv[...].astype(F32)).astype(BF16)

    cells = ROWS_DEV * cols
    gains = gains_ref[...]
    fine_in = layer_norm(dot(block_out, lat_w[0]), gains[0:1]).astype(BF16).astype(F32)
    for row in range(ROWS_DEV):
        fpad[1 + row, 8 : 8 + cols, :] = fine_in[row * cols : (row + 1) * cols]

    def halo(pad, first_row, last_row, inner, index):
        below = last_row + 1
        src_col = pl.multiple_of(inner - (inner - 8) * head, 8)
        dst_col = pl.multiple_of((8 + inner) * head, 8)
        tile = pl.ds(src_col, 8)
        into = pl.ds(dst_col, 8)
        body_cols = pl.ds(8, inner)

        def make(src, dst, place, to_blk, to_head):
            return remote(
                src, dst, halo_send.at[index + place], halo_recv.at[index + place], to_blk, to_head
            )

        span = pl.ds(first_row, last_row - first_row + 1)
        return [
            (None, make(pad.at[span, tile], pad.at[span, into], 0, blk, sib)),
            ("up", make(pad.at[first_row, body_cols], pad.at[below, body_cols], 1, blk - 1, head)),
            ("up", make(pad.at[first_row, tile], pad.at[below, into], 2, blk - 1, sib)),
            ("down", make(pad.at[last_row, body_cols], pad.at[0, body_cols], 3, blk + 1, head)),
            ("down", make(pad.at[last_row, tile], pad.at[0, into], 4, blk + 1, sib)),
        ]

    def guarded(way, action):
        if way is None:
            action()
        else:
            pl.when(has_up if way == "up" else has_down)(action)

    opposite = {None: None, "up": "down", "down": "up"}
    fine_halo = halo(fpad, 1, ROWS_DEV, cols, 0)
    for way, copy in fine_halo:
        guarded(way, copy.start)

    tall = block_out[:cols]
    for row in range(1, ROWS_DEV):
        tall = jnp.maximum(tall, block_out[row * cols : (row + 1) * cols])
    pool_rows = ccol.shape[0]
    at_row = lax.broadcasted_iota(jnp.int32, (pool_rows, cols), 0)
    at_col = lax.broadcasted_iota(jnp.int32, (pool_rows, cols), 1)
    pooled = jnp.maximum(
        dot((at_col == 2 * at_row).astype(F32).astype(BF16), tall),
        dot((at_col == 2 * at_row + 1).astype(F32).astype(BF16), tall),
    ).astype(BF16)
    coarse_cols = cols // 2
    coarse_in = layer_norm(dot(pooled, lat_w[1]), gains[2:3]).astype(BF16).astype(F32)
    cpad[1, 8 : 8 + coarse_cols, :] = coarse_in[:coarse_cols]
    coarse_halo = halo(cpad, 1, 1, coarse_cols, 5)
    for way, copy in coarse_halo:
        guarded(way, copy.start)

    channels = fine_ref.shape[-1]
    for way, copy in fine_halo:
        guarded(opposite[way], copy.wait_recv)
    for a in range(3):
        for b in range(3):
            place = (3 * a + b) * channels
            for row in range(ROWS_DEV):
                fcol[row * cols : (row + 1) * cols, place : place + channels] = fpad[
                    row + a, 7 + b : 7 + b + cols, :
                ].astype(BF16)
    fine_out = layer_norm(dot(fcol[...], conv_w[0]), gains[1:2]).astype(BF16)
    for row in range(ROWS_DEV):
        fine_ref[row] = fine_out[row * cols : (row + 1) * cols]

    for way, copy in coarse_halo:
        guarded(opposite[way], copy.wait_recv)
    for a in range(3):
        for b in range(3):
            place = (3 * a + b) * channels
            ccol[:, place : place + channels] = cpad[a, 7 + b : 7 + b + pool_rows, :].astype(BF16)
    coarse_out = layer_norm(dot(ccol[...], conv_w[1]), gains[3:4]).astype(BF16)
    coarse_ref[0] = coarse_out[:coarse_cols]

    for way, copy in fine_halo + coarse_halo:
        guarded(way, copy.wait_send)
    for sub in range(SUBS):
        ring_copy(0, sub).wait_send()

    def drain(step, carry):
        for sub in range(SUBS):
            sib_copy(step, sub).wait_send()

            @pl.when(step < count - 1)
            def _():
                ring_copy(step, sub).wait_send()

        return carry

    lax.fori_loop(1, count, drain, 0)


def body(tokens, norm_gain, qkv_weight, out_weight, lateral_weight, conv_weight, level_gains):
    count = lax.axis_size("blk")
    rows, wide = tokens.shape
    width = qkv_weight.shape[1]
    heads_width = qkv_weight.shape[2]
    channels = lateral_weight.shape[2]
    per_pair = 2 * HEAD_DIM
    pairs = heads_width // per_pair
    quad = 2 * per_pair
    half = rows // 2
    cols = GW // 2
    cells = ROWS_DEV * cols
    coarse_cols = cols // 2
    pool_rows = -(-coarse_cols // 16) * 16
    conv_depth = 9 * channels
    vmem = pl.BlockSpec(memory_space=pltpu.VMEM)
    hbm = pl.BlockSpec(memory_space=pl.ANY)
    dma = pltpu.SemaphoreType.DMA
    return pl.pallas_call(
        functools.partial(kernel, count),
        out_shape=(
            jax.ShapeDtypeStruct((ROWS_DEV, cols, channels), BF16),
            jax.ShapeDtypeStruct((ROWS_DEV // 2, coarse_cols, channels), BF16),
        ),
        in_specs=[hbm, vmem, hbm, hbm, hbm, hbm, vmem],
        out_specs=(vmem, vmem),
        scratch_shapes=[
            pltpu.VMEM((2, rows, wide), F32),
            pltpu.VMEM(qkv_weight.shape, BF16),
            pltpu.VMEM(out_weight.shape, BF16),
            pltpu.VMEM(lateral_weight.shape, BF16),
            pltpu.VMEM((2, conv_depth, channels), BF16),
            pltpu.VMEM((heads_width, width), BF16),
            pltpu.VMEM((rows, width), BF16),
            pltpu.VMEM((count, SUBS, half // SUBS, width), BF16),
            pltpu.VMEM((count, SUBS, half // SUBS, width), BF16),
            pltpu.VMEM((pairs, 2 * rows, quad), BF16),
            pltpu.VMEM((rows, heads_width), BF16),
            pltpu.VMEM((heads_width, rows), BF16),
            pltpu.VMEM((pairs, per_pair, 2 * rows), F32),
            pltpu.VMEM((pairs, 1, 2 * rows), F32),
            pltpu.VMEM((pairs, 1, 2 * rows), F32),
            pltpu.VMEM((rows, heads_width), BF16),
            pltpu.VMEM((cells, width), BF16),
            pltpu.VMEM((cells, width), BF16),
            pltpu.VMEM((ROWS_DEV + 2, cols + 16, channels), F32),
            pltpu.VMEM((3, pool_rows + 16, channels), F32),
            pltpu.VMEM((cells, conv_depth), BF16),
            pltpu.VMEM((pool_rows, conv_depth), BF16),
            dma((7,)),
            dma((2,)),
            dma((count, SUBS)),
            dma((count, SUBS)),
            dma((count, SUBS)),
            dma((count, SUBS)),
            dma((2,)),
            dma((10,)),
            dma((10,)),
        ],
        compiler_params=pltpu.CompilerParams(
            collective_id=0, has_side_effects=True, vmem_limit_bytes=50 * 1024 * 1024
        ),
    )(
        tokens,
        norm_gain.reshape(1, width),
        qkv_weight,
        out_weight,
        lateral_weight,
        conv_weight.reshape(2, conv_depth, channels),
        level_gains.reshape(4, channels),
    )


def solution(mesh):
    in_specs = (
        P(("groups", "blk"), "head"),
        P(),
        P(None, None, "head"),
        P("head", None),
        P(),
        P(),
        P(),
    )
    out_specs = (P(("groups", "blk"), "head", None), P(("groups", "blk"), "head", None))
    return jax.shard_map(body, mesh=mesh, in_specs=in_specs, out_specs=out_specs, check_vma=False)
```

```python
import functools

import jax
import jax.numpy as jnp
from jax import lax
from jax.experimental import pallas as pl
from jax.experimental.pallas import tpu as pltpu
from jax.sharding import PartitionSpec as P

HEAD_DIM = 64
ROWS_DEV = 2
GW = 96
SUBS = 4
F32 = jnp.float32
BF16 = jnp.bfloat16
NT = (((1,), (1,)), ((), ()))


def layer_norm(values_in, gain_row):
    mean_row = jnp.mean(values_in, axis=-1, keepdims=True)
    centred = values_in - mean_row
    spread = jnp.mean(centred * centred, axis=-1, keepdims=True)
    return centred * lax.rsqrt(spread + 1e-06) * gain_row


def dot(lhs, rhs):
    return jnp.dot(lhs, rhs, preferred_element_type=F32)


def dot_nt(lhs, rhs):
    return lax.dot_general(lhs, rhs, NT, preferred_element_type=F32)


def kernel(
    count,
    tokens_ref, gain_ref, qkv_hbm, out_hbm, lateral_hbm, conv_hbm, gains_ref,
    fine_ref, coarse_ref,
    tok, qkv, out_w, lat_w, conv_w, wvt, normed, ring, other, qbd, kbuf, vbuf,
    acc, peak, total, att, part_send, part_recv, fpad, cpad, fcol, ccol,
    load_sem, tok_sem, ring_send, ring_recv, sib_send, sib_recv, part_sem, halo_send, halo_recv,
):
    blk = lax.axis_index("blk")
    head = lax.axis_index("head")
    sib = 1 - head
    rows = tok.shape[1]
    half = rows // 2
    cols = GW // 2
    pairs = qbd.shape[0]
    pair_rows = qbd.shape[1]

    even = blk % 2 == 0
    up_ring = jnp.where(
        even, jnp.where(blk == count - 2, blk + 1, blk + 2), jnp.where(blk == 1, blk - 1, blk - 2)
    )
    down_ring = jnp.where(
        even, jnp.where(blk == 0, blk + 1, blk - 2), jnp.where(blk == count - 1, blk - 1, blk + 2)
    )
    target = jnp.where(head == 0, up_ring, down_ring)
    source = jnp.where(head == 0, down_ring, up_ring)

    loads = [
        pltpu.make_async_copy(tokens_ref, tok.at[head], load_sem.at[0]),
        pltpu.make_async_copy(qkv_hbm.at[2], qkv.at[2], load_sem.at[1]),
        pltpu.make_async_copy(qkv_hbm.at[0], qkv.at[0], load_sem.at[2]),
        pltpu.make_async_copy(qkv_hbm.at[1], qkv.at[1], load_sem.at[3]),
        pltpu.make_async_copy(out_hbm, out_w, load_sem.at[4]),
        pltpu.make_async_copy(lateral_hbm, lat_w, load_sem.at[5]),
        pltpu.make_async_copy(conv_hbm, conv_w, load_sem.at[6]),
    ]
    for load in loads:
        load.start()

    fpad[...] = jnp.zeros_like(fpad)
    cpad[...] = jnp.zeros_like(cpad)

    barrier = pltpu.get_barrier_semaphore()

    def greet(to_blk, to_head):
        pl.semaphore_signal(barrier, inc=1, device_id={"blk": to_blk, "head": to_head})

    greet(blk, sib)
    greet(target, head)
    greet(source, head)

    has_up = blk > 0
    has_down = blk < count - 1

    @pl.when(has_up)
    def _():
        greet(blk - 1, head)
        greet(blk - 1, sib)

    @pl.when(has_down)
    def _():
        greet(blk + 1, head)
        greet(blk + 1, sib)

    pl.semaphore_wait(barrier, 3 + 2 * has_up.astype(jnp.int32) + 2 * has_down.astype(jnp.int32))

    def remote(src, dst, send, recv, to_blk, to_head):
        return pltpu.make_async_remote_copy(
            src_ref=src, dst_ref=dst, send_sem=send, recv_sem=recv,
            device_id={"blk": to_blk, "head": to_head},
        )

    tok_copy = remote(tokens_ref, tok.at[head], tok_sem.at[0], tok_sem.at[1], blk, sib)
    tok_copy.start()

    acc[...] = jnp.zeros_like(acc)
    total[...] = jnp.zeros_like(total)
    peak[...] = jnp.full(peak.shape, -jnp.inf, F32)

    last = count // 2

    def ring_copy(step, sub):
        return remote(
            ring.at[step, sub], ring.at[step + 1, sub],
            ring_send.at[step, sub], ring_recv.at[step + 1, sub], target, head,
        )

    def sib_copy(step, sub):
        return remote(
            ring.at[step, sub], other.at[step, sub],
            sib_send.at[step, sub], sib_recv.at[step, sub], blk, sib,
        )

    loads[0].wait()
    tok_copy.wait()
    left, right = tok[0], tok[1]
    width = left.shape[1] + right.shape[1]
    mean_row = (
        jnp.sum(left, axis=-1, keepdims=True) + jnp.sum(right, axis=-1, keepdims=True)
    ) / width
    left = left - mean_row
    right = right - mean_row
    spread = (
        jnp.sum(left * left, axis=-1, keepdims=True) + jnp.sum(right * right, axis=-1, keepdims=True)
    ) / width
    scale = lax.rsqrt(spread + 1e-06)
    gain = gain_ref[...]
    wide = left.shape[1]
    normed[:, :wide] = (left * scale * gain[:, :wide]).astype(BF16)
    normed[:, wide:] = (right * scale * gain[:, wide:]).astype(BF16)
    piece = rows // SUBS
    for sub in range(SUBS):
        start = lax.rem(head * half + sub * piece, rows)
        ring[0, sub] = normed[pl.ds(pl.multiple_of(start, 16), piece), :]
    for sub in range(SUBS):
        ring_copy(0, sub).start()

    loads[1].wait()
    wvt[...] = qkv[2].T
    loads[2].wait()
    queries = (dot(normed[...], qkv[0]) * (HEAD_DIM ** -0.5)).astype(BF16)
    per_pair = 2 * HEAD_DIM
    quad = qbd.shape[2]
    lane = lax.broadcasted_iota(jnp.int32, (rows, quad), 1)
    for pair in range(pairs):
        base = pair * per_pair // quad * quad
        block = queries[:, base : base + quad]
        for inner in range(2):
            first = pair * per_pair + inner * HEAD_DIM - base
            keep = (lane >= first) & (lane < first + HEAD_DIM)
            qbd[pair, inner * rows : (inner + 1) * rows, :] = jnp.where(keep, block, jnp.zeros_like(block))
    loads[3].wait()

    def keys_of(chunk):
        kbuf[: chunk.shape[0], :] = dot(chunk, qkv[1]).astype(BF16)

    def values_of(chunk):
        vbuf[:, : chunk.shape[0]] = dot_nt(wvt[...], chunk).astype(BF16)

    def attend(which, keys):
        scores = []
        for pair in which:
            base = pair * per_pair // quad * quad
            scores.append(dot_nt(kbuf[:keys, base : base + quad], qbd[pair]))
        for pair, score in zip(which, scores):
            before = peak[pair]
            now = jnp.maximum(before, jnp.max(score, axis=0, keepdims=True))
            weights = jnp.exp(score - now)
            factor = jnp.exp(before - now)
            peak[pair] = now
            total[pair] = total[pair] * factor + jnp.sum(weights, axis=0, keepdims=True)
            mixed = dot(
                vbuf[pair * per_pair : (pair + 1) * per_pair, :keys], weights.astype(BF16)
            )
            acc[pair] = acc[pair] * factor + mixed

    def own_chunk():
        return ring[0].reshape(rows, width)

    def two_chunks(step):
        return jnp.concatenate(
            [ring[step].reshape(rows, width), other[step].reshape(rows, width)], axis=0
        )

    def last_chunk():
        return jnp.concatenate(
            [
                ring[last, : SUBS // 2].reshape(half, width),
                other[last, : SUBS // 2].reshape(half, width),
            ],
            axis=0,
        )

    def arrive(step, sub):
        ring_copy(step - 1, sub).wait_recv()
        if sub < SUBS // 2:
            @pl.when(step < last)
            def _():
                ring_copy(step, sub).start()
        else:
            @pl.when(step < last - 1)
            def _():
                ring_copy(step, sub).start()
        sib_copy(step, sub).start()

    def met(step, subs):
        for sub in range(subs):
            sib_copy(step, sub).wait_recv()

    low, high = range(pairs // 2), range(pairs // 2, pairs)

    def hop(step, chunk_of, keys):
        arrive(step, 0)
        keys_of(chunk_of())
        arrive(step, 1)
        values_of(chunk_of())
        arrive(step, 2)
        attend(low, keys)
        arrive(step, 3)
        attend(high, keys)

    hop(1, own_chunk, rows)

    def ring_step(step, carry):
        met(step - 1, SUBS)
        hop(step, lambda: two_chunks(step - 1), 2 * rows)
        return carry

    lax.fori_loop(2, last, ring_step, 0)
    met(last - 1, SUBS)
    arrive(last, 0)
    keys_of(two_chunks(last - 1))
    arrive(last, 1)
    values_of(two_chunks(last - 1))
    attend(low, 2 * rows)
    attend(high, 2 * rows)
    met(last, SUBS // 2)
    keys_of(last_chunk())
    values_of(last_chunk())
    attend(range(pairs), rows)

    pair_lane = lax.broadcasted_iota(jnp.int32, (rows, per_pair), 1)
    for pair in range(pairs):
        done = (acc[pair] / total[pair]).T
        att[:, pair * per_pair : (pair + 1) * per_pair] = jnp.where(
            pair_lane < HEAD_DIM, done[:rows], done[rows:]
        ).astype(BF16)

    loads[4].wait()

    def tile_rows(ref, side):
        return jnp.concatenate(
            [
                ref[pl.ds(pl.multiple_of(side * cols + row * GW, 16), cols), :]
                for row in range(ROWS_DEV)
            ],
            axis=0,
        )

    part_send[...] = dot(tile_rows(att, sib), out_w[...]).astype(BF16)
    part_copy = remote(part_send, part_recv, part_sem.at[0], part_sem.at[1], blk, sib)
    part_copy.start()
    own = dot(tile_rows(att, head), out_w[...])
    residual = jnp.concatenate([tile_rows(tok.at[0], head), tile_rows(tok.at[1], head)], axis=1)
    own = own + residual
    loads[5].wait()
    loads[6].wait()
    part_copy.wait()
    block_out = (own + part_recv[...].astype(F32)).astype(BF16)

    cells = ROWS_DEV * cols
    fine_in = layer_norm(dot(block_out, lat_w[0]), gains_ref[0, 0:1]).astype(BF16).astype(F32)
    for row in range(ROWS_DEV):
        fpad[1 + row, 8 : 8 + cols, :] = fine_in[row * cols : (row + 1) * cols]

    def halo(pad, first_row, last_row, inner, index):
        below = last_row + 1
        src_col = pl.multiple_of(inner - (inner - 8) * head, 8)
        dst_col = pl.multiple_of((8 + inner) * head, 8)
        tile = pl.ds(src_col, 8)
        into = pl.ds(dst_col, 8)
        body_cols = pl.ds(8, inner)

        def make(src, dst, place, to_blk, to_head):
            return remote(
                src, dst, halo_send.at[index + place], halo_recv.at[index + place], to_blk, to_head
            )

        span = pl.ds(first_row, last_row - first_row + 1)
        return [
            (None, make(pad.at[span, tile], pad.at[span, into], 0, blk, sib)),
            ("up", make(pad.at[first_row, body_cols], pad.at[below, body_cols], 1, blk - 1, head)),
            ("up", make(pad.at[first_row, tile], pad.at[below, into], 2, blk - 1, sib)),
            ("down", make(pad.at[last_row, body_cols], pad.at[0, body_cols], 3, blk + 1, head)),
            ("down", make(pad.at[last_row, tile], pad.at[0, into], 4, blk + 1, sib)),
        ]

    def guarded(way, action):
        if way is None:
            action()
        else:
            pl.when(has_up if way == "up" else has_down)(action)

    opposite = {None: None, "up": "down", "down": "up"}
    fine_halo = halo(fpad, 1, ROWS_DEV, cols, 0)
    for way, copy in fine_halo:
        guarded(way, copy.start)

    tall = block_out[:cols]
    for row in range(1, ROWS_DEV):
        tall = jnp.maximum(tall, block_out[row * cols : (row + 1) * cols])
    pool_rows = ccol.shape[0]
    at_row = lax.broadcasted_iota(jnp.int32, (pool_rows, cols), 0)
    at_col = lax.broadcasted_iota(jnp.int32, (pool_rows, cols), 1)
    pooled = jnp.maximum(
        dot((at_col == 2 * at_row).astype(F32).astype(BF16), tall),
        dot((at_col == 2 * at_row + 1).astype(F32).astype(BF16), tall),
    ).astype(BF16)
    coarse_cols = cols // 2
    coarse_in = layer_norm(dot(pooled, lat_w[1]), gains_ref[1, 0:1]).astype(BF16).astype(F32)
    cpad[1, 8 : 8 + coarse_cols, :] = coarse_in[:coarse_cols]
    coarse_halo = halo(cpad, 1, 1, coarse_cols, 5)
    for way, copy in coarse_halo:
        guarded(way, copy.start)

    channels = fine_ref.shape[-1]
    for way, copy in fine_halo:
        guarded(opposite[way], copy.wait_recv)
    for a in range(3):
        for b in range(3):
            place = (3 * a + b) * channels
            for row in range(ROWS_DEV):
                fcol[row * cols : (row + 1) * cols, place : place + channels] = fpad[
                    row + a, 7 + b : 7 + b + cols, :
                ].astype(BF16)
    fine_out = layer_norm(dot(fcol[...], conv_w[0]), gains_ref[0, 1:2]).astype(BF16)
    for row in range(ROWS_DEV):
        fine_ref[row] = fine_out[row * cols : (row + 1) * cols]

    for way, copy in coarse_halo:
        guarded(opposite[way], copy.wait_recv)
    for a in range(3):
        for b in range(3):
            place = (3 * a + b) * channels
            ccol[:, place : place + channels] = cpad[a, 7 + b : 7 + b + pool_rows, :].astype(BF16)
    coarse_out = layer_norm(dot(ccol[...], conv_w[1]), gains_ref[1, 1:2]).astype(BF16)
    coarse_ref[0] = coarse_out[:coarse_cols]

    for way, copy in fine_halo + coarse_halo:
        guarded(way, copy.wait_send)
    for sub in range(SUBS):
        ring_copy(0, sub).wait_send()

    def drain(step, carry):
        for sub in range(SUBS):
            sib_copy(step, sub).wait_send()
            if sub < SUBS // 2:
                ring_copy(step, sub).wait_send()
            else:
                @pl.when(step < last - 1)
                def _():
                    ring_copy(step, sub).wait_send()

        return carry

    lax.fori_loop(1, last, drain, 0)
    for sub in range(SUBS // 2):
        sib_copy(last, sub).wait_send()


def body(tokens, norm_gain, qkv_weight, out_weight, lateral_weight, conv_weight, level_gains):
    count = lax.axis_size("blk")
    rows, wide = tokens.shape
    width = qkv_weight.shape[1]
    heads_width = qkv_weight.shape[2]
    channels = lateral_weight.shape[2]
    per_pair = 2 * HEAD_DIM
    pairs = heads_width // per_pair
    quad = 2 * per_pair
    hops = count // 2 + 1
    cols = GW // 2
    cells = ROWS_DEV * cols
    coarse_cols = cols // 2
    pool_rows = -(-coarse_cols // 16) * 16
    conv_depth = 9 * channels
    vmem = pl.BlockSpec(memory_space=pltpu.VMEM)
    hbm = pl.BlockSpec(memory_space=pl.ANY)
    dma = pltpu.SemaphoreType.DMA
    return pl.pallas_call(
        functools.partial(kernel, count),
        out_shape=(
            jax.ShapeDtypeStruct((ROWS_DEV, cols, channels), BF16),
            jax.ShapeDtypeStruct((ROWS_DEV // 2, coarse_cols, channels), BF16),
        ),
        in_specs=[hbm, vmem, hbm, hbm, hbm, hbm, vmem],
        out_specs=(vmem, vmem),
        scratch_shapes=[
            pltpu.VMEM((2, rows, wide), F32),
            pltpu.VMEM(qkv_weight.shape, BF16),
            pltpu.VMEM(out_weight.shape, BF16),
            pltpu.VMEM(lateral_weight.shape, BF16),
            pltpu.VMEM((2, conv_depth, channels), BF16),
            pltpu.VMEM((heads_width, width), BF16),
            pltpu.VMEM((rows, width), BF16),
            pltpu.VMEM((hops, SUBS, rows // SUBS, width), BF16),
            pltpu.VMEM((hops, SUBS, rows // SUBS, width), BF16),
            pltpu.VMEM((pairs, 2 * rows, quad), BF16),
            pltpu.VMEM((2 * rows, heads_width), BF16),
            pltpu.VMEM((heads_width, 2 * rows), BF16),
            pltpu.VMEM((pairs, per_pair, 2 * rows), F32),
            pltpu.VMEM((pairs, 1, 2 * rows), F32),
            pltpu.VMEM((pairs, 1, 2 * rows), F32),
            pltpu.VMEM((rows, heads_width), BF16),
            pltpu.VMEM((cells, width), BF16),
            pltpu.VMEM((cells, width), BF16),
            pltpu.VMEM((ROWS_DEV + 2, cols + 16, channels), F32),
            pltpu.VMEM((3, pool_rows + 16, channels), F32),
            pltpu.VMEM((cells, conv_depth), BF16),
            pltpu.VMEM((pool_rows, conv_depth), BF16),
            dma((7,)),
            dma((2,)),
            dma((hops, SUBS)),
            dma((hops, SUBS)),
            dma((hops, SUBS)),
            dma((hops, SUBS)),
            dma((2,)),
            dma((10,)),
            dma((10,)),
        ],
        compiler_params=pltpu.CompilerParams(
            collective_id=0, has_side_effects=True, vmem_limit_bytes=62 * 1024 * 1024
        ),
    )(
        tokens,
        norm_gain.reshape(1, width),
        qkv_weight,
        out_weight,
        lateral_weight,
        conv_weight.reshape(2, conv_depth, channels),
        level_gains,
    )


def solution(mesh):
    in_specs = (
        P(("groups", "blk"), "head"),
        P(),
        P(None, None, "head"),
        P("head", None),
        P(),
        P(),
        P(),
    )
    out_specs = (P(("groups", "blk"), "head", None), P(("groups", "blk"), "head", None))
    return jax.shard_map(body, mesh=mesh, in_specs=in_specs, out_specs=out_specs, check_vma=False)
```

```python
import functools

import jax
import jax.numpy as jnp
from jax import lax
from jax.experimental import pallas as pl
from jax.experimental.pallas import tpu as pltpu
from jax.sharding import PartitionSpec as P

HEAD_DIM = 64
ROWS_DEV = 2
GW = 96
SUBS = 4
F32 = jnp.float32
BF16 = jnp.bfloat16
NT = (((1,), (1,)), ((), ()))


def layer_norm(values_in, gain_row):
    mean_row = jnp.mean(values_in, axis=-1, keepdims=True)
    centred = values_in - mean_row
    spread = jnp.mean(centred * centred, axis=-1, keepdims=True)
    return centred * lax.rsqrt(spread + 1e-06) * gain_row


def dot(lhs, rhs):
    return jnp.dot(lhs, rhs, preferred_element_type=F32)


def dot_nt(lhs, rhs):
    return lax.dot_general(lhs, rhs, NT, preferred_element_type=F32)


def kernel(
    count,
    tokens_ref, gain_ref, qkv_hbm, out_hbm, lateral_hbm, conv_hbm, gains_ref,
    fine_ref, coarse_ref,
    tok, qkv, out_w, lat_w, conv_w, normed, ring, other, qbd, kbuf, vbuf,
    acc, peak, total, att, part_send, part_recv, fpad, cpad, fcol, ccol,
    load_sem, tok_sem, ring_send, ring_recv, sib_send, sib_recv, part_sem, halo_send, halo_recv,
):
    blk = lax.axis_index("blk")
    head = lax.axis_index("head")
    sib = 1 - head
    rows = tok.shape[1]
    half = rows // 2
    cols = GW // 2
    pairs = qbd.shape[0]
    pair_rows = qbd.shape[1]

    even = blk % 2 == 0
    up_ring = jnp.where(
        even, jnp.where(blk == count - 2, blk + 1, blk + 2), jnp.where(blk == 1, blk - 1, blk - 2)
    )
    down_ring = jnp.where(
        even, jnp.where(blk == 0, blk + 1, blk - 2), jnp.where(blk == count - 1, blk - 1, blk + 2)
    )
    target = jnp.where(head == 0, up_ring, down_ring)
    source = jnp.where(head == 0, down_ring, up_ring)

    loads = [
        pltpu.make_async_copy(tokens_ref, tok.at[head], load_sem.at[0]),
        pltpu.make_async_copy(qkv_hbm.at[0], qkv.at[0], load_sem.at[1]),
        pltpu.make_async_copy(qkv_hbm.at[1], qkv.at[1], load_sem.at[2]),
        pltpu.make_async_copy(qkv_hbm.at[2], qkv.at[2], load_sem.at[3]),
        pltpu.make_async_copy(out_hbm, out_w, load_sem.at[4]),
        pltpu.make_async_copy(lateral_hbm, lat_w, load_sem.at[5]),
        pltpu.make_async_copy(conv_hbm, conv_w, load_sem.at[6]),
    ]
    for load in loads:
        load.start()

    fpad[...] = jnp.zeros_like(fpad)
    cpad[...] = jnp.zeros_like(cpad)

    barrier = pltpu.get_barrier_semaphore()

    def greet(to_blk, to_head):
        pl.semaphore_signal(barrier, inc=1, device_id={"blk": to_blk, "head": to_head})

    greet(blk, sib)
    greet(target, head)
    greet(source, head)

    has_up = blk > 0
    has_down = blk < count - 1

    @pl.when(has_up)
    def _():
        greet(blk - 1, head)
        greet(blk - 1, sib)

    @pl.when(has_down)
    def _():
        greet(blk + 1, head)
        greet(blk + 1, sib)

    pl.semaphore_wait(barrier, 3 + 2 * has_up.astype(jnp.int32) + 2 * has_down.astype(jnp.int32))

    def remote(src, dst, send, recv, to_blk, to_head):
        return pltpu.make_async_remote_copy(
            src_ref=src, dst_ref=dst, send_sem=send, recv_sem=recv,
            device_id={"blk": to_blk, "head": to_head},
        )

    tok_copy = remote(tokens_ref, tok.at[head], tok_sem.at[0], tok_sem.at[1], blk, sib)
    tok_copy.start()

    acc[...] = jnp.zeros_like(acc)
    total[...] = jnp.zeros_like(total)
    peak[...] = jnp.full(peak.shape, -jnp.inf, F32)

    last = count // 2

    def ring_copy(step, sub):
        return remote(
            ring.at[step, sub], ring.at[step + 1, sub],
            ring_send.at[step, sub], ring_recv.at[step + 1, sub], target, head,
        )

    def sib_copy(step, sub):
        return remote(
            ring.at[step, sub], other.at[step, sub],
            sib_send.at[step, sub], sib_recv.at[step, sub], blk, sib,
        )

    loads[0].wait()
    tok_copy.wait()
    left, right = tok[0], tok[1]
    width = left.shape[1] + right.shape[1]
    mean_row = (
        jnp.sum(left, axis=-1, keepdims=True) + jnp.sum(right, axis=-1, keepdims=True)
    ) / width
    left = left - mean_row
    right = right - mean_row
    spread = (
        jnp.sum(left * left, axis=-1, keepdims=True) + jnp.sum(right * right, axis=-1, keepdims=True)
    ) / width
    scale = lax.rsqrt(spread + 1e-06)
    gain = gain_ref[...]
    wide = left.shape[1]
    normed[:, :wide] = (left * scale * gain[:, :wide]).astype(BF16)
    normed[:, wide:] = (right * scale * gain[:, wide:]).astype(BF16)
    piece = rows // SUBS
    for sub in range(SUBS):
        start = lax.rem(head * half + sub * piece, rows)
        ring[0, sub] = normed[pl.ds(pl.multiple_of(start, 16), piece), :]
    for sub in range(SUBS):
        ring_copy(0, sub).start()

    def keys_of(chunk):
        kbuf[: chunk.shape[0], :] = dot(chunk, qkv[1]).astype(BF16)

    def values_of(chunk):
        vbuf[:, : chunk.shape[0]] = dot(chunk, qkv[2]).astype(BF16).T

    def attend(which, keys):
        scores = []
        for pair in which:
            base = pair * per_pair // quad * quad
            scores.append(dot_nt(kbuf[:keys, base : base + quad], qbd[pair]))
        for pair, score in zip(which, scores):
            before = peak[pair]
            now = jnp.maximum(before, jnp.max(score, axis=0, keepdims=True))
            weights = jnp.exp(score - now)
            factor = jnp.exp(before - now)
            peak[pair] = now
            total[pair] = total[pair] * factor + jnp.sum(weights, axis=0, keepdims=True)
            mixed = dot(
                vbuf[pair * per_pair : (pair + 1) * per_pair, :keys], weights.astype(BF16)
            )
            acc[pair] = acc[pair] * factor + mixed

    def own_chunk():
        return ring[0].reshape(rows, width)

    def two_chunks(step):
        return jnp.concatenate(
            [ring[step].reshape(rows, width), other[step].reshape(rows, width)], axis=0
        )

    def last_chunk():
        return jnp.concatenate(
            [
                ring[last, : SUBS // 2].reshape(half, width),
                other[last, : SUBS // 2].reshape(half, width),
            ],
            axis=0,
        )

    def arrive(step, sub):
        ring_copy(step - 1, sub).wait_recv()
        if sub < SUBS // 2:
            @pl.when(step < last)
            def _():
                ring_copy(step, sub).start()
        else:
            @pl.when(step < last - 1)
            def _():
                ring_copy(step, sub).start()
        sib_copy(step, sub).start()

    def met(step, subs):
        for sub in range(subs):
            sib_copy(step, sub).wait_recv()

    low, high = range(pairs // 2), range(pairs // 2, pairs)

    def hop(step, chunk_of, keys):
        arrive(step, 0)
        keys_of(chunk_of())
        arrive(step, 1)
        values_of(chunk_of())
        arrive(step, 2)
        attend(low, keys)
        arrive(step, 3)
        attend(high, keys)

    loads[1].wait()
    queries = (dot(normed[...], qkv[0]) * (HEAD_DIM ** -0.5)).astype(BF16)
    per_pair = 2 * HEAD_DIM
    quad = qbd.shape[2]
    lane = lax.broadcasted_iota(jnp.int32, (rows, quad), 1)
    for pair in range(pairs):
        base = pair * per_pair // quad * quad
        block = queries[:, base : base + quad]
        for inner in range(2):
            first = pair * per_pair + inner * HEAD_DIM - base
            keep = (lane >= first) & (lane < first + HEAD_DIM)
            qbd[pair, inner * rows : (inner + 1) * rows, :] = jnp.where(keep, block, jnp.zeros_like(block))
    arrive(1, 0)
    loads[2].wait()
    keys_of(own_chunk())
    arrive(1, 1)
    loads[3].wait()
    values_of(own_chunk())
    arrive(1, 2)
    attend(low, rows)
    arrive(1, 3)
    attend(high, rows)

    def ring_step(step, carry):
        met(step - 1, SUBS)
        hop(step, lambda: two_chunks(step - 1), 2 * rows)
        return carry

    lax.fori_loop(2, last, ring_step, 0)
    met(last - 1, SUBS)
    arrive(last, 0)
    keys_of(two_chunks(last - 1))
    arrive(last, 1)
    values_of(two_chunks(last - 1))
    attend(low, 2 * rows)
    attend(high, 2 * rows)
    met(last, SUBS // 2)
    keys_of(last_chunk())
    values_of(last_chunk())
    attend(range(pairs), rows)

    pair_lane = lax.broadcasted_iota(jnp.int32, (rows, per_pair), 1)
    for pair in range(pairs):
        done = (acc[pair] / total[pair]).T
        att[:, pair * per_pair : (pair + 1) * per_pair] = jnp.where(
            pair_lane < HEAD_DIM, done[:rows], done[rows:]
        ).astype(BF16)

    loads[4].wait()

    def tile_rows(ref, side):
        return jnp.concatenate(
            [
                ref[pl.ds(pl.multiple_of(side * cols + row * GW, 16), cols), :]
                for row in range(ROWS_DEV)
            ],
            axis=0,
        )

    part_send[...] = dot(tile_rows(att, sib), out_w[...]).astype(BF16)
    part_copy = remote(part_send, part_recv, part_sem.at[0], part_sem.at[1], blk, sib)
    part_copy.start()
    own = dot(tile_rows(att, head), out_w[...])
    residual = jnp.concatenate([tile_rows(tok.at[0], head), tile_rows(tok.at[1], head)], axis=1)
    own = own + residual
    loads[5].wait()
    loads[6].wait()
    part_copy.wait()
    block_out = (own + part_recv[...].astype(F32)).astype(BF16)

    cells = ROWS_DEV * cols
    fine_in = layer_norm(dot(block_out, lat_w[0]), gains_ref[0, 0:1]).astype(BF16).astype(F32)
    for row in range(ROWS_DEV):
        fpad[1 + row, 8 : 8 + cols, :] = fine_in[row * cols : (row + 1) * cols]

    def halo(pad, first_row, last_row, inner, index):
        below = last_row + 1
        src_col = pl.multiple_of(inner - (inner - 8) * head, 8)
        dst_col = pl.multiple_of((8 + inner) * head, 8)
        tile = pl.ds(src_col, 8)
        into = pl.ds(dst_col, 8)
        body_cols = pl.ds(8, inner)

        def make(src, dst, place, to_blk, to_head):
            return remote(
                src, dst, halo_send.at[index + place], halo_recv.at[index + place], to_blk, to_head
            )

        span = pl.ds(first_row, last_row - first_row + 1)
        return [
            (None, make(pad.at[span, tile], pad.at[span, into], 0, blk, sib)),
            ("up", make(pad.at[first_row, body_cols], pad.at[below, body_cols], 1, blk - 1, head)),
            ("up", make(pad.at[first_row, tile], pad.at[below, into], 2, blk - 1, sib)),
            ("down", make(pad.at[last_row, body_cols], pad.at[0, body_cols], 3, blk + 1, head)),
            ("down", make(pad.at[last_row, tile], pad.at[0, into], 4, blk + 1, sib)),
        ]

    def guarded(way, action):
        if way is None:
            action()
        else:
            pl.when(has_up if way == "up" else has_down)(action)

    opposite = {None: None, "up": "down", "down": "up"}
    fine_halo = halo(fpad, 1, ROWS_DEV, cols, 0)
    for way, copy in fine_halo:
        guarded(way, copy.start)

    tall = block_out[:cols]
    for row in range(1, ROWS_DEV):
        tall = jnp.maximum(tall, block_out[row * cols : (row + 1) * cols])
    pool_rows = ccol.shape[0]
    at_row = lax.broadcasted_iota(jnp.int32, (pool_rows, cols), 0)
    at_col = lax.broadcasted_iota(jnp.int32, (pool_rows, cols), 1)
    pooled = jnp.maximum(
        dot((at_col == 2 * at_row).astype(F32).astype(BF16), tall),
        dot((at_col == 2 * at_row + 1).astype(F32).astype(BF16), tall),
    ).astype(BF16)
    coarse_cols = cols // 2
    coarse_in = layer_norm(dot(pooled, lat_w[1]), gains_ref[1, 0:1]).astype(BF16).astype(F32)
    cpad[1, 8 : 8 + coarse_cols, :] = coarse_in[:coarse_cols]
    coarse_halo = halo(cpad, 1, 1, coarse_cols, 5)
    for way, copy in coarse_halo:
        guarded(way, copy.start)

    channels = fine_ref.shape[-1]
    for way, copy in fine_halo:
        guarded(opposite[way], copy.wait_recv)
    for a in range(3):
        for b in range(3):
            place = (3 * a + b) * channels
            for row in range(ROWS_DEV):
                fcol[row * cols : (row + 1) * cols, place : place + channels] = fpad[
                    row + a, 7 + b : 7 + b + cols, :
                ].astype(BF16)
    fine_out = layer_norm(dot(fcol[...], conv_w[0]), gains_ref[0, 1:2]).astype(BF16)
    for row in range(ROWS_DEV):
        fine_ref[row] = fine_out[row * cols : (row + 1) * cols]

    for way, copy in coarse_halo:
        guarded(opposite[way], copy.wait_recv)
    for a in range(3):
        for b in range(3):
            place = (3 * a + b) * channels
            ccol[:, place : place + channels] = cpad[a, 7 + b : 7 + b + pool_rows, :].astype(BF16)
    coarse_out = layer_norm(dot(ccol[...], conv_w[1]), gains_ref[1, 1:2]).astype(BF16)
    coarse_ref[0] = coarse_out[:coarse_cols]

    for way, copy in fine_halo + coarse_halo:
        guarded(way, copy.wait_send)
    for sub in range(SUBS):
        ring_copy(0, sub).wait_send()

    def drain(step, carry):
        for sub in range(SUBS):
            sib_copy(step, sub).wait_send()
            if sub < SUBS // 2:
                ring_copy(step, sub).wait_send()
            else:
                @pl.when(step < last - 1)
                def _():
                    ring_copy(step, sub).wait_send()

        return carry

    lax.fori_loop(1, last, drain, 0)
    for sub in range(SUBS // 2):
        sib_copy(last, sub).wait_send()


def deliver(fine_in, coarse_in, fine_out, coarse_out, sem):
    copies = [
        pltpu.make_async_copy(fine_in, fine_out, sem.at[0]),
        pltpu.make_async_copy(coarse_in, coarse_out, sem.at[1]),
    ]
    for copy in copies:
        copy.start()
    for copy in copies:
        copy.wait()


def body(tokens, norm_gain, qkv_weight, out_weight, lateral_weight, conv_weight, level_gains):
    count = lax.axis_size("blk")
    rows, wide = tokens.shape
    width = qkv_weight.shape[1]
    heads_width = qkv_weight.shape[2]
    channels = lateral_weight.shape[2]
    per_pair = 2 * HEAD_DIM
    pairs = heads_width // per_pair
    quad = 2 * per_pair
    hops = count // 2 + 1
    cols = GW // 2
    cells = ROWS_DEV * cols
    coarse_cols = cols // 2
    pool_rows = -(-coarse_cols // 16) * 16
    conv_depth = 9 * channels
    vmem = pl.BlockSpec(memory_space=pltpu.VMEM)
    hbm = pl.BlockSpec(memory_space=pl.ANY)
    dma = pltpu.SemaphoreType.DMA
    maps = pl.pallas_call(
        functools.partial(kernel, count),
        out_shape=(
            jax.ShapeDtypeStruct((ROWS_DEV, cols, channels), BF16),
            jax.ShapeDtypeStruct((ROWS_DEV // 2, coarse_cols, channels), BF16),
        ),
        in_specs=[hbm, vmem, hbm, hbm, hbm, hbm, vmem],
        out_specs=(vmem, vmem),
        scratch_shapes=[
            pltpu.VMEM((2, rows, wide), F32),
            pltpu.VMEM(qkv_weight.shape, BF16),
            pltpu.VMEM(out_weight.shape, BF16),
            pltpu.VMEM(lateral_weight.shape, BF16),
            pltpu.VMEM((2, conv_depth, channels), BF16),
            pltpu.VMEM((rows, width), BF16),
            pltpu.VMEM((hops, SUBS, rows // SUBS, width), BF16),
            pltpu.VMEM((hops, SUBS, rows // SUBS, width), BF16),
            pltpu.VMEM((pairs, 2 * rows, quad), BF16),
            pltpu.VMEM((2 * rows, heads_width), BF16),
            pltpu.VMEM((heads_width, 2 * rows), BF16),
            pltpu.VMEM((pairs, per_pair, 2 * rows), F32),
            pltpu.VMEM((pairs, 1, 2 * rows), F32),
            pltpu.VMEM((pairs, 1, 2 * rows), F32),
            pltpu.VMEM((rows, heads_width), BF16),
            pltpu.VMEM((cells, width), BF16),
            pltpu.VMEM((cells, width), BF16),
            pltpu.VMEM((ROWS_DEV + 2, cols + 16, channels), F32),
            pltpu.VMEM((3, pool_rows + 16, channels), F32),
            pltpu.VMEM((cells, conv_depth), BF16),
            pltpu.VMEM((pool_rows, conv_depth), BF16),
            dma((7,)),
            dma((2,)),
            dma((hops, SUBS)),
            dma((hops, SUBS)),
            dma((hops, SUBS)),
            dma((hops, SUBS)),
            dma((2,)),
            dma((10,)),
            dma((10,)),
        ],
        compiler_params=pltpu.CompilerParams(
            collective_id=0, has_side_effects=True, vmem_limit_bytes=62 * 1024 * 1024
        ),
    )(
        tokens,
        norm_gain.reshape(1, width),
        qkv_weight,
        out_weight,
        lateral_weight,
        conv_weight.reshape(2, conv_depth, channels),
        level_gains,
    )
    return pl.pallas_call(
        deliver,
        out_shape=tuple(jax.ShapeDtypeStruct(each.shape, each.dtype) for each in maps),
        in_specs=[hbm, hbm],
        out_specs=(hbm, hbm),
        scratch_shapes=[dma((2,))],
    )(*maps)


def solution(mesh):
    in_specs = (
        P(("groups", "blk"), "head"),
        P(),
        P(None, None, "head"),
        P("head", None),
        P(),
        P(),
        P(),
    )
    out_specs = (P(("groups", "blk"), "head", None), P(("groups", "blk"), "head", None))
    return jax.shard_map(body, mesh=mesh, in_specs=in_specs, out_specs=out_specs, check_vma=False)
```

```python
import functools

import jax
import jax.numpy as jnp
from jax import lax
from jax.experimental import pallas as pl
from jax.experimental.pallas import tpu as pltpu
from jax.sharding import PartitionSpec as P

HEAD_DIM = 64
ROWS_DEV = 2
GW = 96
SUBS = 4
F32 = jnp.float32
BF16 = jnp.bfloat16
NT = (((1,), (1,)), ((), ()))


def layer_norm(values_in, gain_row):
    mean_row = jnp.mean(values_in, axis=-1, keepdims=True)
    centred = values_in - mean_row
    spread = jnp.mean(centred * centred, axis=-1, keepdims=True)
    return centred * lax.rsqrt(spread + 1e-06) * gain_row


def dot(lhs, rhs):
    return jnp.dot(lhs, rhs, preferred_element_type=F32)


def dot_nt(lhs, rhs):
    return lax.dot_general(lhs, rhs, NT, preferred_element_type=F32)


def kernel(
    count,
    tokens_ref, gain_ref, qkv_hbm, out_hbm, lateral_hbm, conv_hbm, gains_ref,
    fine_ref, coarse_ref,
    tok, qkv, out_w, lat_w, conv_w, normed, ring, other, qbd, kbuf, vbuf,
    acc, peak, total, att, part_send, part_recv, fpad, cpad, fcol, ccol,
    load_sem, tok_send, tok_recv, ring_send, ring_recv, sib_send, sib_recv, part_sem, halo_send, halo_recv,
):
    blk = lax.axis_index("blk")
    head = lax.axis_index("head")
    sib = 1 - head
    rows = tok.shape[1]
    half = rows // 2
    cols = GW // 2
    pairs = qbd.shape[0]
    pair_rows = qbd.shape[1]

    even = blk % 2 == 0
    up_ring = jnp.where(
        even, jnp.where(blk == count - 2, blk + 1, blk + 2), jnp.where(blk == 1, blk - 1, blk - 2)
    )
    down_ring = jnp.where(
        even, jnp.where(blk == 0, blk + 1, blk - 2), jnp.where(blk == count - 1, blk - 1, blk + 2)
    )
    target = jnp.where(head == 0, up_ring, down_ring)
    source = jnp.where(head == 0, down_ring, up_ring)

    piece = rows // SUBS

    def piece_rows(side, sub):
        start = lax.rem(side * half + sub * piece, rows)
        return pl.ds(pl.multiple_of(start, 16), piece)

    loads = [
        pltpu.make_async_copy(
            tokens_ref.at[piece_rows(head, sub)], tok.at[head, piece_rows(head, sub)],
            load_sem.at[6 + sub],
        )
        for sub in range(SUBS)
    ]
    weights_in = [
        pltpu.make_async_copy(qkv_hbm.at[0], qkv.at[0], load_sem.at[0]),
        pltpu.make_async_copy(qkv_hbm.at[1], qkv.at[1], load_sem.at[1]),
        pltpu.make_async_copy(qkv_hbm.at[2], qkv.at[2], load_sem.at[2]),
        pltpu.make_async_copy(out_hbm, out_w, load_sem.at[3]),
        pltpu.make_async_copy(lateral_hbm, lat_w, load_sem.at[4]),
        pltpu.make_async_copy(conv_hbm, conv_w, load_sem.at[5]),
    ]
    for load in loads + weights_in:
        load.start()

    fpad[...] = jnp.zeros_like(fpad)
    cpad[...] = jnp.zeros_like(cpad)

    barrier = pltpu.get_barrier_semaphore()

    def greet(to_blk, to_head):
        pl.semaphore_signal(barrier, inc=1, device_id={"blk": to_blk, "head": to_head})

    greet(blk, sib)
    greet(target, head)
    greet(source, head)

    has_up = blk > 0
    has_down = blk < count - 1

    @pl.when(has_up)
    def _():
        greet(blk - 1, head)
        greet(blk - 1, sib)

    @pl.when(has_down)
    def _():
        greet(blk + 1, head)
        greet(blk + 1, sib)

    pl.semaphore_wait(barrier, 3 + 2 * has_up.astype(jnp.int32) + 2 * has_down.astype(jnp.int32))

    def remote(src, dst, send, recv, to_blk, to_head):
        return pltpu.make_async_remote_copy(
            src_ref=src, dst_ref=dst, send_sem=send, recv_sem=recv,
            device_id={"blk": to_blk, "head": to_head},
        )

    tok_out = [
        remote(
            tokens_ref.at[piece_rows(sib, sub)], tok.at[head, piece_rows(sib, sub)],
            tok_send.at[sub], tok_recv.at[sub], blk, sib,
        )
        for sub in range(SUBS)
    ]
    for copy in tok_out:
        copy.start()
    tok_in = [
        remote(
            tokens_ref.at[piece_rows(head, sub)], tok.at[sib, piece_rows(head, sub)],
            tok_send.at[sub], tok_recv.at[sub], blk, sib,
        )
        for sub in range(SUBS)
    ]

    acc[...] = jnp.zeros_like(acc)
    total[...] = jnp.zeros_like(total)
    peak[...] = jnp.full(peak.shape, -jnp.inf, F32)

    last = count // 2

    def ring_copy(step, sub):
        return remote(
            ring.at[step, sub], ring.at[step + 1, sub],
            ring_send.at[step, sub], ring_recv.at[step + 1, sub], target, head,
        )

    def sib_copy(step, sub):
        return remote(
            ring.at[step, sub], other.at[step, sub],
            sib_send.at[step, sub], sib_recv.at[step, sub], blk, sib,
        )

    gain = gain_ref[...]
    wide = tok.shape[2]
    width = 2 * wide
    for sub in range(SUBS):
        here = piece_rows(head, sub)
        loads[sub].wait()
        tok_in[sub].wait_recv()
        left, right = tok[0, here, :], tok[1, here, :]
        mean_row = (
            jnp.sum(left, axis=-1, keepdims=True) + jnp.sum(right, axis=-1, keepdims=True)
        ) / width
        left = left - mean_row
        right = right - mean_row
        spread = (
            jnp.sum(left * left, axis=-1, keepdims=True)
            + jnp.sum(right * right, axis=-1, keepdims=True)
        ) / width
        scale = lax.rsqrt(spread + 1e-06)
        ring[0, sub, :, :wide] = (left * scale * gain[:, :wide]).astype(BF16)
        ring[0, sub, :, wide:] = (right * scale * gain[:, wide:]).astype(BF16)
        ring_copy(0, sub).start()
    for sub in range(SUBS):
        normed[piece_rows(head, sub), :] = ring[0, sub]

    def keys_of(chunk):
        kbuf[: chunk.shape[0], :] = dot(chunk, qkv[1]).astype(BF16)

    def values_of(chunk):
        vbuf[:, : chunk.shape[0]] = dot(chunk, qkv[2]).astype(BF16).T

    def attend(which, keys):
        scores = []
        for pair in which:
            base = pair * per_pair // quad * quad
            scores.append(dot_nt(kbuf[:keys, base : base + quad], qbd[pair]))
        for pair, score in zip(which, scores):
            before = peak[pair]
            now = jnp.maximum(before, jnp.max(score, axis=0, keepdims=True))
            weights = jnp.exp(score - now)
            factor = jnp.exp(before - now)
            peak[pair] = now
            total[pair] = total[pair] * factor + jnp.sum(weights, axis=0, keepdims=True)
            mixed = dot(
                vbuf[pair * per_pair : (pair + 1) * per_pair, :keys], weights.astype(BF16)
            )
            acc[pair] = acc[pair] * factor + mixed

    def own_chunk():
        return ring[0].reshape(rows, width)

    def two_chunks(step):
        return jnp.concatenate(
            [ring[step].reshape(rows, width), other[step].reshape(rows, width)], axis=0
        )

    def part_chunk(step, first):
        subs = slice(first, first + SUBS // 2)
        return jnp.concatenate(
            [ring[step, subs].reshape(half, width), other[step, subs].reshape(half, width)], axis=0
        )

    def arrive(step, sub):
        ring_copy(step - 1, sub).wait_recv()
        if sub < SUBS // 2:
            @pl.when(step < last)
            def _():
                ring_copy(step, sub).start()
        else:
            @pl.when(step < last - 1)
            def _():
                ring_copy(step, sub).start()
        sib_copy(step, sub).start()

    def met(step, first, past):
        for sub in range(first, past):
            sib_copy(step, sub).wait_recv()

    low, high = range(pairs // 2), range(pairs // 2, pairs)

    def hop(step, chunk_of, keys):
        arrive(step, 0)
        keys_of(chunk_of())
        arrive(step, 1)
        values_of(chunk_of())
        arrive(step, 2)
        attend(low, keys)
        arrive(step, 3)
        attend(high, keys)

    weights_in[0].wait()
    queries = (dot(normed[...], qkv[0]) * (HEAD_DIM ** -0.5)).astype(BF16)
    per_pair = 2 * HEAD_DIM
    quad = qbd.shape[2]
    lane = lax.broadcasted_iota(jnp.int32, (rows, quad), 1)
    for pair in range(pairs):
        base = pair * per_pair // quad * quad
        block = queries[:, base : base + quad]
        for inner in range(2):
            first = pair * per_pair + inner * HEAD_DIM - base
            keep = (lane >= first) & (lane < first + HEAD_DIM)
            qbd[pair, inner * rows : (inner + 1) * rows, :] = jnp.where(keep, block, jnp.zeros_like(block))
    arrive(1, 0)
    weights_in[1].wait()
    keys_of(own_chunk())
    arrive(1, 1)
    weights_in[2].wait()
    values_of(own_chunk())
    arrive(1, 2)
    attend(low, rows)
    arrive(1, 3)
    attend(high, rows)

    def ring_step(step, carry):
        met(step - 1, 0, SUBS)
        hop(step, lambda: two_chunks(step - 1), 2 * rows)
        return carry

    lax.fori_loop(2, last, ring_step, 0)
    mid = SUBS // 2
    met(last - 1, 0, mid)
    keys_of(part_chunk(last - 1, 0))
    values_of(part_chunk(last - 1, 0))
    attend(range(pairs), rows)
    arrive(last, 0)
    met(last - 1, mid, SUBS)
    keys_of(part_chunk(last - 1, mid))
    values_of(part_chunk(last - 1, mid))
    arrive(last, 1)
    attend(range(pairs), rows)
    met(last, 0, mid)
    keys_of(part_chunk(last, 0))
    values_of(part_chunk(last, 0))
    attend(range(pairs), rows)

    pair_lane = lax.broadcasted_iota(jnp.int32, (rows, per_pair), 1)
    for pair in range(pairs):
        done = (acc[pair] / total[pair]).T
        att[:, pair * per_pair : (pair + 1) * per_pair] = jnp.where(
            pair_lane < HEAD_DIM, done[:rows], done[rows:]
        ).astype(BF16)

    weights_in[3].wait()

    def tile_rows(ref, side):
        return jnp.concatenate(
            [
                ref[pl.ds(pl.multiple_of(side * cols + row * GW, 16), cols), :]
                for row in range(ROWS_DEV)
            ],
            axis=0,
        )

    part_send[...] = dot(tile_rows(att, sib), out_w[...]).astype(BF16)
    part_copy = remote(part_send, part_recv, part_sem.at[0], part_sem.at[1], blk, sib)
    part_copy.start()
    own = dot(tile_rows(att, head), out_w[...])
    residual = jnp.concatenate([tile_rows(tok.at[0], head), tile_rows(tok.at[1], head)], axis=1)
    own = own + residual
    weights_in[4].wait()
    weights_in[5].wait()
    part_copy.wait()
    block_out = (own + part_recv[...].astype(F32)).astype(BF16)

    cells = ROWS_DEV * cols
    fine_in = layer_norm(dot(block_out, lat_w[0]), gains_ref[0, 0:1]).astype(BF16).astype(F32)
    for row in range(ROWS_DEV):
        fpad[1 + row, 8 : 8 + cols, :] = fine_in[row * cols : (row + 1) * cols]

    def halo(pad, first_row, last_row, inner, index):
        below = last_row + 1
        src_col = pl.multiple_of(inner - (inner - 8) * head, 8)
        dst_col = pl.multiple_of((8 + inner) * head, 8)
        tile = pl.ds(src_col, 8)
        into = pl.ds(dst_col, 8)
        body_cols = pl.ds(8, inner)

        def make(src, dst, place, to_blk, to_head):
            return remote(
                src, dst, halo_send.at[index + place], halo_recv.at[index + place], to_blk, to_head
            )

        span = pl.ds(first_row, last_row - first_row + 1)
        return [
            (None, make(pad.at[span, tile], pad.at[span, into], 0, blk, sib)),
            ("up", make(pad.at[first_row, body_cols], pad.at[below, body_cols], 1, blk - 1, head)),
            ("up", make(pad.at[first_row, tile], pad.at[below, into], 2, blk - 1, sib)),
            ("down", make(pad.at[last_row, body_cols], pad.at[0, body_cols], 3, blk + 1, head)),
            ("down", make(pad.at[last_row, tile], pad.at[0, into], 4, blk + 1, sib)),
        ]

    def guarded(way, action):
        if way is None:
            action()
        else:
            pl.when(has_up if way == "up" else has_down)(action)

    opposite = {None: None, "up": "down", "down": "up"}
    fine_halo = halo(fpad, 1, ROWS_DEV, cols, 0)
    for way, copy in fine_halo:
        guarded(way, copy.start)

    tall = block_out[:cols]
    for row in range(1, ROWS_DEV):
        tall = jnp.maximum(tall, block_out[row * cols : (row + 1) * cols])
    pool_rows = ccol.shape[0]
    at_row = lax.broadcasted_iota(jnp.int32, (pool_rows, cols), 0)
    at_col = lax.broadcasted_iota(jnp.int32, (pool_rows, cols), 1)
    pooled = jnp.maximum(
        dot((at_col == 2 * at_row).astype(F32).astype(BF16), tall),
        dot((at_col == 2 * at_row + 1).astype(F32).astype(BF16), tall),
    ).astype(BF16)
    coarse_cols = cols // 2
    coarse_in = layer_norm(dot(pooled, lat_w[1]), gains_ref[1, 0:1]).astype(BF16).astype(F32)
    cpad[1, 8 : 8 + coarse_cols, :] = coarse_in[:coarse_cols]
    coarse_halo = halo(cpad, 1, 1, coarse_cols, 5)
    for way, copy in coarse_halo:
        guarded(way, copy.start)

    channels = fine_ref.shape[-1]
    for way, copy in fine_halo:
        guarded(opposite[way], copy.wait_recv)
    for a in range(3):
        for b in range(3):
            place = (3 * a + b) * channels
            for row in range(ROWS_DEV):
                fcol[row * cols : (row + 1) * cols, place : place + channels] = fpad[
                    row + a, 7 + b : 7 + b + cols, :
                ].astype(BF16)
    fine_out = layer_norm(dot(fcol[...], conv_w[0]), gains_ref[0, 1:2]).astype(BF16)
    for row in range(ROWS_DEV):
        fine_ref[row] = fine_out[row * cols : (row + 1) * cols]

    for way, copy in coarse_halo:
        guarded(opposite[way], copy.wait_recv)
    for a in range(3):
        for b in range(3):
            place = (3 * a + b) * channels
            ccol[:, place : place + channels] = cpad[a, 7 + b : 7 + b + pool_rows, :].astype(BF16)
    coarse_out = layer_norm(dot(ccol[...], conv_w[1]), gains_ref[1, 1:2]).astype(BF16)
    coarse_ref[0] = coarse_out[:coarse_cols]

    for way, copy in fine_halo + coarse_halo:
        guarded(way, copy.wait_send)
    for sub in range(SUBS):
        tok_out[sub].wait_send()
        ring_copy(0, sub).wait_send()

    def drain(step, carry):
        for sub in range(SUBS):
            sib_copy(step, sub).wait_send()
            if sub < SUBS // 2:
                ring_copy(step, sub).wait_send()
            else:
                @pl.when(step < last - 1)
                def _():
                    ring_copy(step, sub).wait_send()

        return carry

    lax.fori_loop(1, last, drain, 0)
    for sub in range(SUBS // 2):
        sib_copy(last, sub).wait_send()


def body(tokens, norm_gain, qkv_weight, out_weight, lateral_weight, conv_weight, level_gains):
    count = lax.axis_size("blk")
    rows, wide = tokens.shape
    width = qkv_weight.shape[1]
    heads_width = qkv_weight.shape[2]
    channels = lateral_weight.shape[2]
    per_pair = 2 * HEAD_DIM
    pairs = heads_width // per_pair
    quad = 2 * per_pair
    hops = count // 2 + 1
    cols = GW // 2
    cells = ROWS_DEV * cols
    coarse_cols = cols // 2
    pool_rows = -(-coarse_cols // 16) * 16
    conv_depth = 9 * channels
    vmem = pl.BlockSpec(memory_space=pltpu.VMEM)
    hbm = pl.BlockSpec(memory_space=pl.ANY)
    dma = pltpu.SemaphoreType.DMA
    return pl.pallas_call(
        functools.partial(kernel, count),
        out_shape=(
            jax.ShapeDtypeStruct((ROWS_DEV, cols, channels), BF16),
            jax.ShapeDtypeStruct((ROWS_DEV // 2, coarse_cols, channels), BF16),
        ),
        in_specs=[hbm, vmem, hbm, hbm, hbm, hbm, vmem],
        out_specs=(vmem, vmem),
        scratch_shapes=[
            pltpu.VMEM((2, rows, wide), F32),
            pltpu.VMEM(qkv_weight.shape, BF16),
            pltpu.VMEM(out_weight.shape, BF16),
            pltpu.VMEM(lateral_weight.shape, BF16),
            pltpu.VMEM((2, conv_depth, channels), BF16),
            pltpu.VMEM((rows, width), BF16),
            pltpu.VMEM((hops, SUBS, rows // SUBS, width), BF16),
            pltpu.VMEM((hops, SUBS, rows // SUBS, width), BF16),
            pltpu.VMEM((pairs, 2 * rows, quad), BF16),
            pltpu.VMEM((2 * rows, heads_width), BF16),
            pltpu.VMEM((heads_width, 2 * rows), BF16),
            pltpu.VMEM((pairs, per_pair, 2 * rows), F32),
            pltpu.VMEM((pairs, 1, 2 * rows), F32),
            pltpu.VMEM((pairs, 1, 2 * rows), F32),
            pltpu.VMEM((rows, heads_width), BF16),
            pltpu.VMEM((cells, width), BF16),
            pltpu.VMEM((cells, width), BF16),
            pltpu.VMEM((ROWS_DEV + 2, cols + 16, channels), F32),
            pltpu.VMEM((3, pool_rows + 16, channels), F32),
            pltpu.VMEM((cells, conv_depth), BF16),
            pltpu.VMEM((pool_rows, conv_depth), BF16),
            dma((6 + SUBS,)),
            dma((SUBS,)),
            dma((SUBS,)),
            dma((hops, SUBS)),
            dma((hops, SUBS)),
            dma((hops, SUBS)),
            dma((hops, SUBS)),
            dma((2,)),
            dma((10,)),
            dma((10,)),
        ],
        compiler_params=pltpu.CompilerParams(
            collective_id=0, has_side_effects=True, vmem_limit_bytes=54912 * 1024
        ),
    )(
        tokens,
        norm_gain.reshape(1, width),
        qkv_weight,
        out_weight,
        lateral_weight,
        conv_weight.reshape(2, conv_depth, channels),
        level_gains,
    )


def solution(mesh):
    in_specs = (
        P(("groups", "blk"), "head"),
        P(),
        P(None, None, "head"),
        P("head", None),
        P(),
        P(),
        P(),
    )
    out_specs = (P(("groups", "blk"), "head", None), P(("groups", "blk"), "head", None))
    return jax.shard_map(body, mesh=mesh, in_specs=in_specs, out_specs=out_specs, check_vma=False)
```

```python
import functools

import jax
import jax.numpy as jnp
from jax import lax
from jax.experimental import pallas as pl
from jax.experimental.pallas import tpu as pltpu
from jax.sharding import PartitionSpec as P

HEAD_DIM = 64
ROWS_DEV = 2
GW = 96
SUBS = 4
F32 = jnp.float32
BF16 = jnp.bfloat16
NT = (((1,), (1,)), ((), ()))


def layer_norm(values_in, gain_row):
    mean_row = jnp.mean(values_in, axis=-1, keepdims=True)
    centred = values_in - mean_row
    spread = jnp.mean(centred * centred, axis=-1, keepdims=True)
    return centred * lax.rsqrt(spread + 1e-06) * gain_row


def dot(lhs, rhs):
    return jnp.dot(lhs, rhs, preferred_element_type=F32)


def dot_nt(lhs, rhs):
    return lax.dot_general(lhs, rhs, NT, preferred_element_type=F32)


def kernel(
    count,
    tokens_ref, gain_hbm, qkv_hbm, out_hbm, lateral_hbm, conv_hbm, gains_hbm,
    fine_ref, coarse_ref,
    gain_ref, gains_ref, tok, qkv, out_w, lat_w, conv_w, normed, ring, other, qbd, kbuf, vbuf,
    acc, peak, total, att, part_send, part_recv, fpad, cpad, fcol, ccol,
    load_sem, tok_send, tok_recv, ring_send, ring_recv, sib_send, sib_recv, part_sem, halo_send, halo_recv,
):
    blk = lax.axis_index("blk")
    head = lax.axis_index("head")
    sib = 1 - head
    rows = tok.shape[1]
    half = rows // 2
    cols = GW // 2
    pairs = qbd.shape[0]
    pair_rows = qbd.shape[1]

    even = blk % 2 == 0
    up_ring = jnp.where(
        even, jnp.where(blk == count - 2, blk + 1, blk + 2), jnp.where(blk == 1, blk - 1, blk - 2)
    )
    down_ring = jnp.where(
        even, jnp.where(blk == 0, blk + 1, blk - 2), jnp.where(blk == count - 1, blk - 1, blk + 2)
    )
    target = jnp.where(head == 0, up_ring, down_ring)
    source = jnp.where(head == 0, down_ring, up_ring)

    piece = rows // SUBS

    def piece_rows(side, sub):
        start = lax.rem(side * half + sub * piece, rows)
        return pl.ds(pl.multiple_of(start, 16), piece)

    loads = [
        pltpu.make_async_copy(
            tokens_ref.at[piece_rows(head, sub)], tok.at[head, piece_rows(head, sub)],
            load_sem.at[6 + sub],
        )
        for sub in range(SUBS)
    ]
    weights_in = [
        pltpu.make_async_copy(qkv_hbm.at[0], qkv.at[0], load_sem.at[0]),
        pltpu.make_async_copy(qkv_hbm.at[1], qkv.at[1], load_sem.at[1]),
        pltpu.make_async_copy(qkv_hbm.at[2], qkv.at[2], load_sem.at[2]),
        pltpu.make_async_copy(out_hbm, out_w, load_sem.at[3]),
        pltpu.make_async_copy(lateral_hbm, lat_w, load_sem.at[4]),
        pltpu.make_async_copy(conv_hbm, conv_w, load_sem.at[5]),
        pltpu.make_async_copy(gains_hbm, gains_ref, load_sem.at[6 + SUBS]),
        pltpu.make_async_copy(gain_hbm, gain_ref, load_sem.at[7 + SUBS]),
    ]
    for load in loads + weights_in:
        load.start()

    fpad[...] = jnp.zeros_like(fpad)
    cpad[...] = jnp.zeros_like(cpad)

    barrier = pltpu.get_barrier_semaphore()

    def greet(to_blk, to_head):
        pl.semaphore_signal(barrier, inc=1, device_id={"blk": to_blk, "head": to_head})

    greet(blk, sib)
    greet(target, head)
    greet(source, head)

    has_up = blk > 0
    has_down = blk < count - 1

    @pl.when(has_up)
    def _():
        greet(blk - 1, head)
        greet(blk - 1, sib)

    @pl.when(has_down)
    def _():
        greet(blk + 1, head)
        greet(blk + 1, sib)

    pl.semaphore_wait(barrier, 3 + 2 * has_up.astype(jnp.int32) + 2 * has_down.astype(jnp.int32))

    def remote(src, dst, send, recv, to_blk, to_head):
        return pltpu.make_async_remote_copy(
            src_ref=src, dst_ref=dst, send_sem=send, recv_sem=recv,
            device_id={"blk": to_blk, "head": to_head},
        )

    tok_out = [
        remote(
            tokens_ref.at[piece_rows(sib, sub)], tok.at[head, piece_rows(sib, sub)],
            tok_send.at[sub], tok_recv.at[sub], blk, sib,
        )
        for sub in range(SUBS)
    ]
    for copy in tok_out:
        copy.start()
    tok_in = [
        remote(
            tokens_ref.at[piece_rows(head, sub)], tok.at[sib, piece_rows(head, sub)],
            tok_send.at[sub], tok_recv.at[sub], blk, sib,
        )
        for sub in range(SUBS)
    ]

    acc[...] = jnp.zeros_like(acc)
    total[...] = jnp.zeros_like(total)
    peak[...] = jnp.full(peak.shape, -jnp.inf, F32)

    last = count // 2

    class Together:
        def __init__(self, copies):
            self.copies = copies

        def start(self):
            for copy in self.copies:
                copy.start()

        def wait_send(self):
            for copy in self.copies:
                copy.wait_send()

        def wait_recv(self):
            for copy in self.copies:
                copy.wait_recv()

    def ring_copy(step, sub):
        copies = []
        for side in range(2):
            span = pl.ds(side * tok.shape[2], tok.shape[2])
            copies.append(
                remote(
                    ring.at[step, sub, :, span], ring.at[step + 1, sub, :, span],
                    ring_send.at[step, sub, side], ring_recv.at[step + 1, sub, side], target, head,
                )
            )
        return Together(copies)

    def sib_copy(step, sub):
        return remote(
            ring.at[step, sub], other.at[step, sub],
            sib_send.at[step, sub], sib_recv.at[step, sub], blk, sib,
        )

    weights_in[7].wait()
    gain = gain_ref[...]
    wide = tok.shape[2]
    width = 2 * wide
    for sub in range(SUBS):
        here = piece_rows(head, sub)
        loads[sub].wait()
        tok_in[sub].wait_recv()
        left, right = tok[0, here, :], tok[1, here, :]
        mean_row = (
            jnp.sum(left, axis=-1, keepdims=True) + jnp.sum(right, axis=-1, keepdims=True)
        ) / width
        left = left - mean_row
        right = right - mean_row
        spread = (
            jnp.sum(left * left, axis=-1, keepdims=True)
            + jnp.sum(right * right, axis=-1, keepdims=True)
        ) / width
        scale = lax.rsqrt(spread + 1e-06)
        ring[0, sub, :, :wide] = (left * scale * gain[:, :wide]).astype(BF16)
        ring[0, sub, :, wide:] = (right * scale * gain[:, wide:]).astype(BF16)
        ring_copy(0, sub).start()
    for sub in range(SUBS):
        normed[piece_rows(head, sub), :] = ring[0, sub]

    def keys_of(chunk):
        kbuf[: chunk.shape[0], :] = dot(chunk, qkv[1]).astype(BF16)

    def values_of(chunk):
        vbuf[:, : chunk.shape[0]] = dot(chunk, qkv[2]).astype(BF16).T

    def attend(which, keys):
        scores = []
        for pair in which:
            base = pair * per_pair // quad * quad
            scores.append(dot_nt(kbuf[:keys, base : base + quad], qbd[pair]))
        for pair, score in zip(which, scores):
            before = peak[pair]
            now = jnp.maximum(before, jnp.max(score, axis=0, keepdims=True))
            weights = jnp.exp(score - now)
            factor = jnp.exp(before - now)
            peak[pair] = now
            total[pair] = total[pair] * factor + jnp.sum(weights, axis=0, keepdims=True)
            mixed = dot(
                vbuf[pair * per_pair : (pair + 1) * per_pair, :keys], weights.astype(BF16)
            )
            acc[pair] = acc[pair] * factor + mixed

    def own_chunk():
        return ring[0].reshape(rows, width)

    def two_chunks(step):
        return jnp.concatenate(
            [ring[step].reshape(rows, width), other[step].reshape(rows, width)], axis=0
        )

    def part_chunk(step, first):
        subs = slice(first, first + SUBS // 2)
        return jnp.concatenate(
            [ring[step, subs].reshape(half, width), other[step, subs].reshape(half, width)], axis=0
        )

    def arrive(step, sub):
        ring_copy(step - 1, sub).wait_recv()
        if sub < SUBS // 2:
            @pl.when(step < last)
            def _():
                ring_copy(step, sub).start()
        else:
            @pl.when(step < last - 1)
            def _():
                ring_copy(step, sub).start()
        sib_copy(step, sub).start()

    def met(step, first, past):
        for sub in range(first, past):
            sib_copy(step, sub).wait_recv()

    low, high = range(pairs // 2), range(pairs // 2, pairs)

    def hop(step, chunk_of, keys):
        arrive(step, 0)
        keys_of(chunk_of())
        arrive(step, 1)
        values_of(chunk_of())
        arrive(step, 2)
        attend(low, keys)
        arrive(step, 3)
        attend(high, keys)

    weights_in[0].wait()
    queries = (dot(normed[...], qkv[0]) * (HEAD_DIM ** -0.5)).astype(BF16)
    per_pair = 2 * HEAD_DIM
    quad = qbd.shape[2]
    lane = lax.broadcasted_iota(jnp.int32, (rows, quad), 1)
    for pair in range(pairs):
        base = pair * per_pair // quad * quad
        block = queries[:, base : base + quad]
        for inner in range(2):
            first = pair * per_pair + inner * HEAD_DIM - base
            keep = (lane >= first) & (lane < first + HEAD_DIM)
            qbd[pair, inner * rows : (inner + 1) * rows, :] = jnp.where(keep, block, jnp.zeros_like(block))
    arrive(1, 0)
    weights_in[1].wait()
    keys_of(own_chunk())
    arrive(1, 1)
    weights_in[2].wait()
    values_of(own_chunk())
    arrive(1, 2)
    attend(low, rows)
    arrive(1, 3)
    attend(high, rows)

    def ring_step(step, carry):
        met(step - 1, 0, SUBS)
        hop(step, lambda: two_chunks(step - 1), 2 * rows)
        return carry

    lax.fori_loop(2, last, ring_step, 0)
    mid = SUBS // 2
    met(last - 1, 0, mid)
    keys_of(part_chunk(last - 1, 0))
    values_of(part_chunk(last - 1, 0))
    attend(range(pairs), rows)
    arrive(last, 0)
    met(last - 1, mid, SUBS)
    keys_of(part_chunk(last - 1, mid))
    values_of(part_chunk(last - 1, mid))
    arrive(last, 1)
    attend(range(pairs), rows)
    met(last, 0, mid)
    keys_of(part_chunk(last, 0))
    values_of(part_chunk(last, 0))
    attend(range(pairs), rows)

    pair_lane = lax.broadcasted_iota(jnp.int32, (rows, per_pair), 1)
    for pair in range(pairs):
        done = (acc[pair] / total[pair]).T
        att[:, pair * per_pair : (pair + 1) * per_pair] = jnp.where(
            pair_lane < HEAD_DIM, done[:rows], done[rows:]
        ).astype(BF16)

    weights_in[3].wait()

    def tile_rows(ref, side):
        return jnp.concatenate(
            [
                ref[pl.ds(pl.multiple_of(side * cols + row * GW, 16), cols), :]
                for row in range(ROWS_DEV)
            ],
            axis=0,
        )

    part_send[...] = dot(tile_rows(att, sib), out_w[...]).astype(BF16)
    part_copy = remote(part_send, part_recv, part_sem.at[0], part_sem.at[1], blk, sib)
    part_copy.start()
    own = dot(tile_rows(att, head), out_w[...])
    residual = jnp.concatenate([tile_rows(tok.at[0], head), tile_rows(tok.at[1], head)], axis=1)
    own = own + residual
    weights_in[4].wait()
    weights_in[5].wait()
    weights_in[6].wait()
    part_copy.wait()
    block_out = (own + part_recv[...].astype(F32)).astype(BF16)

    cells = ROWS_DEV * cols
    fine_in = layer_norm(dot(block_out, lat_w[0]), gains_ref[0, 0:1]).astype(BF16).astype(F32)
    for row in range(ROWS_DEV):
        fpad[1 + row, 8 : 8 + cols, :] = fine_in[row * cols : (row + 1) * cols]

    def halo(pad, first_row, last_row, inner, index):
        below = last_row + 1
        src_col = pl.multiple_of(inner - (inner - 8) * head, 8)
        dst_col = pl.multiple_of((8 + inner) * head, 8)
        tile = pl.ds(src_col, 8)
        into = pl.ds(dst_col, 8)
        body_cols = pl.ds(8, inner)

        def make(src, dst, place, to_blk, to_head):
            return remote(
                src, dst, halo_send.at[index + place], halo_recv.at[index + place], to_blk, to_head
            )

        span = pl.ds(first_row, last_row - first_row + 1)
        return [
            (None, make(pad.at[span, tile], pad.at[span, into], 0, blk, sib)),
            ("up", make(pad.at[first_row, body_cols], pad.at[below, body_cols], 1, blk - 1, head)),
            ("up", make(pad.at[first_row, tile], pad.at[below, into], 2, blk - 1, sib)),
            ("down", make(pad.at[last_row, body_cols], pad.at[0, body_cols], 3, blk + 1, head)),
            ("down", make(pad.at[last_row, tile], pad.at[0, into], 4, blk + 1, sib)),
        ]

    def guarded(way, action):
        if way is None:
            action()
        else:
            pl.when(has_up if way == "up" else has_down)(action)

    opposite = {None: None, "up": "down", "down": "up"}
    fine_halo = halo(fpad, 1, ROWS_DEV, cols, 0)
    for way, copy in fine_halo:
        guarded(way, copy.start)

    tall = block_out[:cols]
    for row in range(1, ROWS_DEV):
        tall = jnp.maximum(tall, block_out[row * cols : (row + 1) * cols])
    pool_rows = ccol.shape[0]
    at_row = lax.broadcasted_iota(jnp.int32, (pool_rows, cols), 0)
    at_col = lax.broadcasted_iota(jnp.int32, (pool_rows, cols), 1)
    pooled = jnp.maximum(
        dot((at_col == 2 * at_row).astype(F32).astype(BF16), tall),
        dot((at_col == 2 * at_row + 1).astype(F32).astype(BF16), tall),
    ).astype(BF16)
    coarse_cols = cols // 2
    coarse_in = layer_norm(dot(pooled, lat_w[1]), gains_ref[1, 0:1]).astype(BF16).astype(F32)
    cpad[1, 8 : 8 + coarse_cols, :] = coarse_in[:coarse_cols]
    coarse_halo = halo(cpad, 1, 1, coarse_cols, 5)
    for way, copy in coarse_halo:
        guarded(way, copy.start)

    channels = fine_ref.shape[-1]
    for way, copy in fine_halo:
        guarded(opposite[way], copy.wait_recv)
    for a in range(3):
        for b in range(3):
            place = (3 * a + b) * channels
            for row in range(ROWS_DEV):
                fcol[row * cols : (row + 1) * cols, place : place + channels] = fpad[
                    row + a, 7 + b : 7 + b + cols, :
                ].astype(BF16)
    fine_out = layer_norm(dot(fcol[...], conv_w[0]), gains_ref[0, 1:2]).astype(BF16)
    for row in range(ROWS_DEV):
        fine_ref[row] = fine_out[row * cols : (row + 1) * cols]

    for way, copy in coarse_halo:
        guarded(opposite[way], copy.wait_recv)
    for a in range(3):
        for b in range(3):
            place = (3 * a + b) * channels
            ccol[:, place : place + channels] = cpad[a, 7 + b : 7 + b + pool_rows, :].astype(BF16)
    coarse_out = layer_norm(dot(ccol[...], conv_w[1]), gains_ref[1, 1:2]).astype(BF16)
    coarse_ref[0] = coarse_out[:coarse_cols]

    for way, copy in fine_halo + coarse_halo:
        guarded(way, copy.wait_send)
    for sub in range(SUBS):
        tok_out[sub].wait_send()
        ring_copy(0, sub).wait_send()

    def drain(step, carry):
        for sub in range(SUBS):
            sib_copy(step, sub).wait_send()
            if sub < SUBS // 2:
                ring_copy(step, sub).wait_send()
            else:
                @pl.when(step < last - 1)
                def _():
                    ring_copy(step, sub).wait_send()

        return carry

    lax.fori_loop(1, last, drain, 0)
    for sub in range(SUBS // 2):
        sib_copy(last, sub).wait_send()


def body(tokens, norm_gain, qkv_weight, out_weight, lateral_weight, conv_weight, level_gains):
    count = lax.axis_size("blk")
    rows, wide = tokens.shape
    width = qkv_weight.shape[1]
    heads_width = qkv_weight.shape[2]
    channels = lateral_weight.shape[2]
    per_pair = 2 * HEAD_DIM
    pairs = heads_width // per_pair
    quad = 2 * per_pair
    hops = count // 2 + 1
    cols = GW // 2
    cells = ROWS_DEV * cols
    coarse_cols = cols // 2
    pool_rows = -(-coarse_cols // 16) * 16
    conv_depth = 9 * channels
    vmem = pl.BlockSpec(memory_space=pltpu.VMEM)
    hbm = pl.BlockSpec(memory_space=pl.ANY)
    dma = pltpu.SemaphoreType.DMA
    return pl.pallas_call(
        functools.partial(kernel, count),
        out_shape=(
            jax.ShapeDtypeStruct((ROWS_DEV, cols, channels), BF16),
            jax.ShapeDtypeStruct((ROWS_DEV // 2, coarse_cols, channels), BF16),
        ),
        in_specs=[hbm] * 7,
        out_specs=(vmem, vmem),
        scratch_shapes=[
            pltpu.VMEM((1, width), F32),
            pltpu.VMEM(level_gains.shape, F32),
            pltpu.VMEM((2, rows, wide), F32),
            pltpu.VMEM(qkv_weight.shape, BF16),
            pltpu.VMEM(out_weight.shape, BF16),
            pltpu.VMEM(lateral_weight.shape, BF16),
            pltpu.VMEM((2, conv_depth, channels), BF16),
            pltpu.VMEM((rows, width), BF16),
            pltpu.VMEM((hops, SUBS, rows // SUBS, width), BF16),
            pltpu.VMEM((hops, SUBS, rows // SUBS, width), BF16),
            pltpu.VMEM((pairs, 2 * rows, quad), BF16),
            pltpu.VMEM((2 * rows, heads_width), BF16),
            pltpu.VMEM((heads_width, 2 * rows), BF16),
            pltpu.VMEM((pairs, per_pair, 2 * rows), F32),
            pltpu.VMEM((pairs, 1, 2 * rows), F32),
            pltpu.VMEM((pairs, 1, 2 * rows), F32),
            pltpu.VMEM((rows, heads_width), BF16),
            pltpu.VMEM((cells, width), BF16),
            pltpu.VMEM((cells, width), BF16),
            pltpu.VMEM((ROWS_DEV + 2, cols + 16, channels), F32),
            pltpu.VMEM((3, pool_rows + 16, channels), F32),
            pltpu.VMEM((cells, conv_depth), BF16),
            pltpu.VMEM((pool_rows, conv_depth), BF16),
            dma((8 + SUBS,)),
            dma((SUBS,)),
            dma((SUBS,)),
            dma((hops, SUBS, 2)),
            dma((hops, SUBS, 2)),
            dma((hops, SUBS)),
            dma((hops, SUBS)),
            dma((2,)),
            dma((10,)),
            dma((10,)),
        ],
        compiler_params=pltpu.CompilerParams(
            collective_id=0, has_side_effects=True, vmem_limit_bytes=54912 * 1024
        ),
    )(
        tokens,
        norm_gain.reshape(1, width),
        qkv_weight,
        out_weight,
        lateral_weight,
        conv_weight.reshape(2, conv_depth, channels),
        level_gains,
    )


def solution(mesh):
    in_specs = (
        P(("groups", "blk"), "head"),
        P(),
        P(None, None, "head"),
        P("head", None),
        P(),
        P(),
        P(),
    )
    out_specs = (P(("groups", "blk"), "head", None), P(("groups", "blk"), "head", None))
    return jax.shard_map(body, mesh=mesh, in_specs=in_specs, out_specs=out_specs, check_vma=False)
```

```python
import functools

import jax
import jax.numpy as jnp
from jax import lax
from jax.experimental import pallas as pl
from jax.experimental.pallas import tpu as pltpu
from jax.sharding import PartitionSpec as P

HEAD_DIM = 64
ROWS_DEV = 2
GW = 96
SUBS = 4
F32 = jnp.float32
BF16 = jnp.bfloat16


def layer_norm(values_in, gain_row):
    mean_row = jnp.mean(values_in, axis=-1, keepdims=True)
    centred = values_in - mean_row
    spread = jnp.mean(centred * centred, axis=-1, keepdims=True)
    return centred * lax.rsqrt(spread + 1e-06) * gain_row


def dot(lhs, rhs):
    return jnp.dot(lhs, rhs, preferred_element_type=F32)


def kernel(
    count,
    tokens_ref, gain_ref, qkv_hbm, out_hbm, lateral_hbm, conv_hbm, gains_ref,
    fine_ref, coarse_ref,
    tok, qkv, out_w, lat_w, conv_w, normed, ring, other, qbd, kbuf, vbuf,
    acc, peak, total, att, part_send, part_recv, fpad, cpad, fcol, ccol,
    load_sem, tok_send, tok_recv, ring_send, ring_recv, sib_send, sib_recv, part_sem, halo_send, halo_recv,
):
    blk = lax.axis_index("blk")
    head = lax.axis_index("head")
    sib = 1 - head
    rows = tok.shape[1]
    half = rows // 2
    cols = GW // 2
    pairs = qbd.shape[0]

    even = blk % 2 == 0
    up_ring = jnp.where(
        even, jnp.where(blk == count - 2, blk + 1, blk + 2), jnp.where(blk == 1, blk - 1, blk - 2)
    )
    down_ring = jnp.where(
        even, jnp.where(blk == 0, blk + 1, blk - 2), jnp.where(blk == count - 1, blk - 1, blk + 2)
    )
    target = jnp.where(head == 0, up_ring, down_ring)
    source = jnp.where(head == 0, down_ring, up_ring)

    piece = rows // SUBS

    def piece_rows(side, sub):
        start = lax.rem(side * half + sub * piece, rows)
        return pl.ds(pl.multiple_of(start, 16), piece)

    loads = [
        pltpu.make_async_copy(
            tokens_ref.at[piece_rows(head, sub)], tok.at[head, piece_rows(head, sub)],
            load_sem.at[6 + sub],
        )
        for sub in range(SUBS)
    ]
    weights_in = [
        pltpu.make_async_copy(qkv_hbm.at[0], qkv.at[0], load_sem.at[0]),
        pltpu.make_async_copy(qkv_hbm.at[1], qkv.at[1], load_sem.at[1]),
        pltpu.make_async_copy(qkv_hbm.at[2], qkv.at[2], load_sem.at[2]),
        pltpu.make_async_copy(out_hbm, out_w, load_sem.at[3]),
        pltpu.make_async_copy(lateral_hbm, lat_w, load_sem.at[4]),
        pltpu.make_async_copy(conv_hbm, conv_w, load_sem.at[5]),
    ]
    for load in loads + weights_in:
        load.start()

    fpad[...] = jnp.zeros_like(fpad)
    cpad[...] = jnp.zeros_like(cpad)

    barrier = pltpu.get_barrier_semaphore()

    def greet(to_blk, to_head):
        pl.semaphore_signal(barrier, inc=1, device_id={"blk": to_blk, "head": to_head})

    greet(blk, sib)
    greet(target, head)
    greet(source, head)

    has_up = blk > 0
    has_down = blk < count - 1

    @pl.when(has_up)
    def _():
        greet(blk - 1, head)
        greet(blk - 1, sib)

    @pl.when(has_down)
    def _():
        greet(blk + 1, head)
        greet(blk + 1, sib)

    pl.semaphore_wait(barrier, 3 + 2 * has_up.astype(jnp.int32) + 2 * has_down.astype(jnp.int32))

    def remote(src, dst, send, recv, to_blk, to_head):
        return pltpu.make_async_remote_copy(
            src_ref=src, dst_ref=dst, send_sem=send, recv_sem=recv,
            device_id={"blk": to_blk, "head": to_head},
        )

    tok_out = [
        remote(
            tokens_ref.at[piece_rows(sib, sub)], tok.at[head, piece_rows(sib, sub)],
            tok_send.at[sub], tok_recv.at[sub], blk, sib,
        )
        for sub in range(SUBS)
    ]
    for copy in tok_out:
        copy.start()
    tok_in = [
        remote(
            tokens_ref.at[piece_rows(head, sub)], tok.at[sib, piece_rows(head, sub)],
            tok_send.at[sub], tok_recv.at[sub], blk, sib,
        )
        for sub in range(SUBS)
    ]

    acc[...] = jnp.zeros_like(acc)
    total[...] = jnp.zeros_like(total)
    peak[...] = jnp.full(peak.shape, -jnp.inf, F32)

    last = count // 2

    def ring_copy(step, sub):
        return remote(
            ring.at[step, sub], ring.at[step + 1, sub],
            ring_send.at[step, sub], ring_recv.at[step + 1, sub], target, head,
        )

    def sib_copy(step, sub):
        return remote(
            ring.at[step, sub], other.at[step, sub],
            sib_send.at[step, sub], sib_recv.at[step, sub], blk, sib,
        )

    gain = gain_ref[...]
    wide = tok.shape[2]
    width = 2 * wide
    for sub in range(SUBS):
        here = piece_rows(head, sub)
        loads[sub].wait()
        tok_in[sub].wait_recv()
        left, right = tok[0, here, :], tok[1, here, :]
        mean_row = (
            jnp.sum(left, axis=-1, keepdims=True) + jnp.sum(right, axis=-1, keepdims=True)
        ) / width
        left = left - mean_row
        right = right - mean_row
        spread = (
            jnp.sum(left * left, axis=-1, keepdims=True)
            + jnp.sum(right * right, axis=-1, keepdims=True)
        ) / width
        scale = lax.rsqrt(spread + 1e-06)
        ring[0, sub, :, :wide] = (left * scale * gain[:, :wide]).astype(BF16)
        ring[0, sub, :, wide:] = (right * scale * gain[:, wide:]).astype(BF16)
        ring_copy(0, sub).start()
    for sub in range(SUBS):
        normed[piece_rows(head, sub), :] = ring[0, sub]

    def keys_of(chunk):
        kbuf[: chunk.shape[0], :] = dot(chunk, qkv[1]).astype(BF16)

    def values_of(chunk):
        vbuf[:, : chunk.shape[0]] = dot(chunk, qkv[2]).astype(BF16).T

    def attend(which, keys):
        scores = []
        for pair in which:
            base = pair * per_pair // quad * quad
            scores.append(dot(kbuf[:keys, base : base + quad], qbd[pair]))
        for pair, score in zip(which, scores):
            before = peak[pair]
            now = jnp.maximum(before, jnp.max(score, axis=0, keepdims=True))
            weights = jnp.exp(score - now)
            factor = jnp.exp(before - now)
            peak[pair] = now
            total[pair] = total[pair] * factor + jnp.sum(weights, axis=0, keepdims=True)
            mixed = dot(
                vbuf[pair * per_pair : (pair + 1) * per_pair, :keys], weights.astype(BF16)
            )
            acc[pair] = acc[pair] * factor + mixed

    def own_chunk():
        return ring[0].reshape(rows, width)

    def two_chunks(step):
        return jnp.concatenate(
            [ring[step].reshape(rows, width), other[step].reshape(rows, width)], axis=0
        )

    def part_chunk(step, first):
        subs = slice(first, first + SUBS // 2)
        return jnp.concatenate(
            [ring[step, subs].reshape(half, width), other[step, subs].reshape(half, width)], axis=0
        )

    def arrive(step, sub):
        ring_copy(step - 1, sub).wait_recv()
        if sub < SUBS // 2:
            @pl.when(step < last)
            def _():
                ring_copy(step, sub).start()
        else:
            @pl.when(step < last - 1)
            def _():
                ring_copy(step, sub).start()
        sib_copy(step, sub).start()

    def met(step, first, past):
        for sub in range(first, past):
            sib_copy(step, sub).wait_recv()

    low, high = range(pairs // 2), range(pairs // 2, pairs)

    def hop(step, chunk_of, keys):
        arrive(step, 0)
        keys_of(chunk_of())
        arrive(step, 1)
        values_of(chunk_of())
        arrive(step, 2)
        attend(low, keys)
        arrive(step, 3)
        attend(high, keys)

    weights_in[0].wait()
    queries = (dot(normed[...], qkv[0]) * (HEAD_DIM ** -0.5)).astype(BF16)
    per_pair = 2 * HEAD_DIM
    quad = qbd.shape[1]
    lane = lax.broadcasted_iota(jnp.int32, (rows, quad), 1)
    for pair in range(pairs):
        base = pair * per_pair // quad * quad
        block = queries[:, base : base + quad]
        both = []
        for inner in range(2):
            first = pair * per_pair + inner * HEAD_DIM - base
            keep = (lane >= first) & (lane < first + HEAD_DIM)
            both.append(jnp.where(keep, block, jnp.zeros_like(block)))
        qbd[pair] = jnp.concatenate(both, axis=0).T
    arrive(1, 0)
    weights_in[1].wait()
    keys_of(own_chunk())
    arrive(1, 1)
    weights_in[2].wait()
    values_of(own_chunk())
    arrive(1, 2)
    attend(low, rows)
    arrive(1, 3)
    attend(high, rows)

    def ring_step(step, carry):
        met(step - 1, 0, SUBS)
        hop(step, lambda: two_chunks(step - 1), 2 * rows)
        return carry

    lax.fori_loop(2, last, ring_step, 0)
    mid = SUBS // 2
    met(last - 1, 0, mid)
    keys_of(part_chunk(last - 1, 0))
    values_of(part_chunk(last - 1, 0))
    attend(range(pairs), rows)
    arrive(last, 0)
    met(last - 1, mid, SUBS)
    keys_of(part_chunk(last - 1, mid))
    values_of(part_chunk(last - 1, mid))
    arrive(last, 1)
    attend(range(pairs), rows)
    met(last, 0, mid)
    keys_of(part_chunk(last, 0))
    values_of(part_chunk(last, 0))
    attend(range(pairs), rows)

    pair_lane = lax.broadcasted_iota(jnp.int32, (rows, per_pair), 1)
    for pair in range(pairs):
        done = (acc[pair] * (1.0 / total[pair])).astype(BF16).T
        att[:, pair * per_pair : (pair + 1) * per_pair] = jnp.where(
            pair_lane < HEAD_DIM, done[:rows], done[rows:]
        )

    weights_in[3].wait()

    def tile_rows(ref, side):
        return jnp.concatenate(
            [
                ref[pl.ds(pl.multiple_of(side * cols + row * GW, 16), cols), :]
                for row in range(ROWS_DEV)
            ],
            axis=0,
        )

    part_send[...] = dot(tile_rows(att, sib), out_w[...]).astype(BF16)
    part_copy = remote(part_send, part_recv, part_sem.at[0], part_sem.at[1], blk, sib)
    part_copy.start()
    own = dot(tile_rows(att, head), out_w[...])
    residual = jnp.concatenate([tile_rows(tok.at[0], head), tile_rows(tok.at[1], head)], axis=1)
    own = own + residual
    weights_in[4].wait()
    weights_in[5].wait()
    part_copy.wait()
    block_out = (own + part_recv[...].astype(F32)).astype(BF16)

    cells = ROWS_DEV * cols
    fine_in = layer_norm(dot(block_out, lat_w[0]), gains_ref[0, 0:1]).astype(BF16).astype(F32)
    for row in range(ROWS_DEV):
        fpad[1 + row, 8 : 8 + cols, :] = fine_in[row * cols : (row + 1) * cols]

    def halo(pad, first_row, last_row, inner, index):
        below = last_row + 1
        src_col = pl.multiple_of(inner - (inner - 8) * head, 8)
        dst_col = pl.multiple_of((8 + inner) * head, 8)
        tile = pl.ds(src_col, 8)
        into = pl.ds(dst_col, 8)
        body_cols = pl.ds(8, inner)

        def make(src, dst, place, to_blk, to_head):
            return remote(
                src, dst, halo_send.at[index + place], halo_recv.at[index + place], to_blk, to_head
            )

        span = pl.ds(first_row, last_row - first_row + 1)
        return [
            (None, make(pad.at[span, tile], pad.at[span, into], 0, blk, sib)),
            ("up", make(pad.at[first_row, body_cols], pad.at[below, body_cols], 1, blk - 1, head)),
            ("up", make(pad.at[first_row, tile], pad.at[below, into], 2, blk - 1, sib)),
            ("down", make(pad.at[last_row, body_cols], pad.at[0, body_cols], 3, blk + 1, head)),
            ("down", make(pad.at[last_row, tile], pad.at[0, into], 4, blk + 1, sib)),
        ]

    def guarded(way, action):
        if way is None:
            action()
        else:
            pl.when(has_up if way == "up" else has_down)(action)

    opposite = {None: None, "up": "down", "down": "up"}
    fine_halo = halo(fpad, 1, ROWS_DEV, cols, 0)
    for way, copy in fine_halo:
        guarded(way, copy.start)

    tall = block_out[:cols]
    for row in range(1, ROWS_DEV):
        tall = jnp.maximum(tall, block_out[row * cols : (row + 1) * cols])
    pool_rows = ccol.shape[0]
    at_row = lax.broadcasted_iota(jnp.int32, (pool_rows, cols), 0)
    at_col = lax.broadcasted_iota(jnp.int32, (pool_rows, cols), 1)
    pooled = jnp.maximum(
        dot((at_col == 2 * at_row).astype(F32).astype(BF16), tall),
        dot((at_col == 2 * at_row + 1).astype(F32).astype(BF16), tall),
    ).astype(BF16)
    coarse_cols = cols // 2
    coarse_in = layer_norm(dot(pooled, lat_w[1]), gains_ref[1, 0:1]).astype(BF16).astype(F32)
    cpad[1, 8 : 8 + coarse_cols, :] = coarse_in[:coarse_cols]
    coarse_halo = halo(cpad, 1, 1, coarse_cols, 5)
    for way, copy in coarse_halo:
        guarded(way, copy.start)

    channels = fine_ref.shape[-1]
    for way, copy in fine_halo:
        guarded(opposite[way], copy.wait_recv)
    for a in range(3):
        for b in range(3):
            place = (3 * a + b) * channels
            for row in range(ROWS_DEV):
                fcol[row * cols : (row + 1) * cols, place : place + channels] = fpad[
                    row + a, 7 + b : 7 + b + cols, :
                ].astype(BF16)
    fine_out = layer_norm(dot(fcol[...], conv_w[0]), gains_ref[0, 1:2]).astype(BF16)
    for row in range(ROWS_DEV):
        fine_ref[row] = fine_out[row * cols : (row + 1) * cols]

    for way, copy in coarse_halo:
        guarded(opposite[way], copy.wait_recv)
    for a in range(3):
        for b in range(3):
            place = (3 * a + b) * channels
            ccol[:, place : place + channels] = cpad[a, 7 + b : 7 + b + pool_rows, :].astype(BF16)
    coarse_out = layer_norm(dot(ccol[...], conv_w[1]), gains_ref[1, 1:2]).astype(BF16)
    coarse_ref[0] = coarse_out[:coarse_cols]

    for way, copy in fine_halo + coarse_halo:
        guarded(way, copy.wait_send)
    for sub in range(SUBS):
        tok_out[sub].wait_send()
        ring_copy(0, sub).wait_send()

    def drain(step, carry):
        for sub in range(SUBS):
            sib_copy(step, sub).wait_send()
            if sub < SUBS // 2:
                ring_copy(step, sub).wait_send()
            else:
                @pl.when(step < last - 1)
                def _():
                    ring_copy(step, sub).wait_send()

        return carry

    lax.fori_loop(1, last, drain, 0)
    for sub in range(SUBS // 2):
        sib_copy(last, sub).wait_send()


def body(tokens, norm_gain, qkv_weight, out_weight, lateral_weight, conv_weight, level_gains):
    count = lax.axis_size("blk")
    rows, wide = tokens.shape
    width = qkv_weight.shape[1]
    heads_width = qkv_weight.shape[2]
    channels = lateral_weight.shape[2]
    per_pair = 2 * HEAD_DIM
    pairs = heads_width // per_pair
    quad = 2 * per_pair
    hops = count // 2 + 1
    cols = GW // 2
    cells = ROWS_DEV * cols
    coarse_cols = cols // 2
    pool_rows = -(-coarse_cols // 16) * 16
    conv_depth = 9 * channels
    vmem = pl.BlockSpec(memory_space=pltpu.VMEM)
    hbm = pl.BlockSpec(memory_space=pl.ANY)
    dma = pltpu.SemaphoreType.DMA
    return pl.pallas_call(
        functools.partial(kernel, count),
        out_shape=(
            jax.ShapeDtypeStruct((ROWS_DEV, cols, channels), BF16),
            jax.ShapeDtypeStruct((ROWS_DEV // 2, coarse_cols, channels), BF16),
        ),
        in_specs=[hbm, vmem, hbm, hbm, hbm, hbm, vmem],
        out_specs=(vmem, vmem),
        scratch_shapes=[
            pltpu.VMEM((2, rows, wide), F32),
            pltpu.VMEM(qkv_weight.shape, BF16),
            pltpu.VMEM(out_weight.shape, BF16),
            pltpu.VMEM(lateral_weight.shape, BF16),
            pltpu.VMEM((2, conv_depth, channels), BF16),
            pltpu.VMEM((rows, width), BF16),
            pltpu.VMEM((hops, SUBS, rows // SUBS, width), BF16),
            pltpu.VMEM((hops, SUBS, rows // SUBS, width), BF16),
            pltpu.VMEM((pairs, quad, 2 * rows), BF16),
            pltpu.VMEM((2 * rows, heads_width), BF16),
            pltpu.VMEM((heads_width, 2 * rows), BF16),
            pltpu.VMEM((pairs, per_pair, 2 * rows), F32),
            pltpu.VMEM((pairs, 1, 2 * rows), F32),
            pltpu.VMEM((pairs, 1, 2 * rows), F32),
            pltpu.VMEM((rows, heads_width), BF16),
            pltpu.VMEM((cells, width), BF16),
            pltpu.VMEM((cells, width), BF16),
            pltpu.VMEM((ROWS_DEV + 2, cols + 16, channels), F32),
            pltpu.VMEM((3, pool_rows + 16, channels), F32),
            pltpu.VMEM((cells, conv_depth), BF16),
            pltpu.VMEM((pool_rows, conv_depth), BF16),
            dma((6 + SUBS,)),
            dma((SUBS,)),
            dma((SUBS,)),
            dma((hops, SUBS)),
            dma((hops, SUBS)),
            dma((hops, SUBS)),
            dma((hops, SUBS)),
            dma((2,)),
            dma((10,)),
            dma((10,)),
        ],
        compiler_params=pltpu.CompilerParams(
            collective_id=0, has_side_effects=True, vmem_limit_bytes=54912 * 1024
        ),
    )(
        tokens,
        norm_gain.reshape(1, width),
        qkv_weight,
        out_weight,
        lateral_weight,
        conv_weight.reshape(2, conv_depth, channels),
        level_gains,
    )


def solution(mesh):
    in_specs = (
        P(("groups", "blk"), "head"),
        P(),
        P(None, None, "head"),
        P("head", None),
        P(),
        P(),
        P(),
    )
    out_specs = (P(("groups", "blk"), "head", None), P(("groups", "blk"), "head", None))
    return jax.shard_map(body, mesh=mesh, in_specs=in_specs, out_specs=out_specs, check_vma=False)
```

```python
import functools

import jax
import jax.numpy as jnp
from jax import lax
from jax.experimental import pallas as pl
from jax.experimental.pallas import tpu as pltpu
from jax.sharding import PartitionSpec as P

HEAD_DIM = 64
ROWS_DEV = 2
GW = 96
SUBS = 4
F32 = jnp.float32
BF16 = jnp.bfloat16


def layer_norm(values_in, gain_row):
    mean_row = jnp.mean(values_in, axis=-1, keepdims=True)
    centred = values_in - mean_row
    spread = jnp.mean(centred * centred, axis=-1, keepdims=True)
    return centred * lax.rsqrt(spread + 1e-06) * gain_row


def dot(lhs, rhs):
    return jnp.dot(lhs, rhs, preferred_element_type=F32)


def kernel(
    count,
    tokens_ref, gain_ref, qkv_hbm, out_hbm, lateral_hbm, conv_hbm, gains_ref,
    fine_ref, coarse_ref,
    tok, qkv, out_w, lat_w, conv_w, normed, ring, other, qbd, kbuf, vbuf,
    acc, peak, total, att, part_send, part_recv, fpad, cpad, fcol, ccol,
    load_sem, tok_send, tok_recv, ring_send, ring_recv, sib_send, sib_recv, part_sem, halo_send, halo_recv,
):
    blk = lax.axis_index("blk")
    head = lax.axis_index("head")
    sib = 1 - head
    rows = tok.shape[1]
    half = rows // 2
    cols = GW // 2
    pairs = qbd.shape[0]

    even = blk % 2 == 0
    up_ring = jnp.where(
        even, jnp.where(blk == count - 2, blk + 1, blk + 2), jnp.where(blk == 1, blk - 1, blk - 2)
    )
    down_ring = jnp.where(
        even, jnp.where(blk == 0, blk + 1, blk - 2), jnp.where(blk == count - 1, blk - 1, blk + 2)
    )
    target = jnp.where(head == 0, up_ring, down_ring)
    source = jnp.where(head == 0, down_ring, up_ring)

    piece = rows // SUBS

    def piece_rows(side, sub):
        start = lax.rem(side * half + sub * piece, rows)
        return pl.ds(pl.multiple_of(start, 16), piece)

    loads = [
        pltpu.make_async_copy(
            tokens_ref.at[piece_rows(head, sub)], tok.at[head, piece_rows(head, sub)],
            load_sem.at[6 + sub],
        )
        for sub in range(SUBS)
    ]
    weights_in = [
        pltpu.make_async_copy(qkv_hbm.at[0], qkv.at[0], load_sem.at[0]),
        pltpu.make_async_copy(qkv_hbm.at[1], qkv.at[1], load_sem.at[1]),
        pltpu.make_async_copy(qkv_hbm.at[2], qkv.at[2], load_sem.at[2]),
        pltpu.make_async_copy(out_hbm, out_w, load_sem.at[3]),
        pltpu.make_async_copy(lateral_hbm, lat_w, load_sem.at[4]),
        pltpu.make_async_copy(conv_hbm, conv_w, load_sem.at[5]),
    ]
    for load in loads + weights_in:
        load.start()

    fpad[...] = jnp.zeros_like(fpad)
    cpad[...] = jnp.zeros_like(cpad)

    barrier = pltpu.get_barrier_semaphore()

    def greet(to_blk, to_head):
        pl.semaphore_signal(barrier, inc=1, device_id={"blk": to_blk, "head": to_head})

    greet(blk, sib)
    greet(target, head)
    greet(source, head)

    has_up = blk > 0
    has_down = blk < count - 1

    @pl.when(has_up)
    def _():
        greet(blk - 1, head)
        greet(blk - 1, sib)

    @pl.when(has_down)
    def _():
        greet(blk + 1, head)
        greet(blk + 1, sib)

    pl.semaphore_wait(barrier, 3 + 2 * has_up.astype(jnp.int32) + 2 * has_down.astype(jnp.int32))

    def remote(src, dst, send, recv, to_blk, to_head):
        return pltpu.make_async_remote_copy(
            src_ref=src, dst_ref=dst, send_sem=send, recv_sem=recv,
            device_id={"blk": to_blk, "head": to_head},
        )

    tok_out = [
        remote(
            tokens_ref.at[piece_rows(sib, sub)], tok.at[head, piece_rows(sib, sub)],
            tok_send.at[sub], tok_recv.at[sub], blk, sib,
        )
        for sub in range(SUBS)
    ]
    for copy in tok_out:
        copy.start()
    tok_in = [
        remote(
            tokens_ref.at[piece_rows(head, sub)], tok.at[sib, piece_rows(head, sub)],
            tok_send.at[sub], tok_recv.at[sub], blk, sib,
        )
        for sub in range(SUBS)
    ]

    acc[...] = jnp.zeros_like(acc)
    total[...] = jnp.zeros_like(total)
    peak[...] = jnp.full(peak.shape, -jnp.inf, F32)

    last = count // 2

    def ring_copy(step, sub):
        return remote(
            ring.at[step, sub], ring.at[step + 1, sub],
            ring_send.at[step, sub], ring_recv.at[step + 1, sub], target, head,
        )

    def sib_copy(step, sub):
        return remote(
            ring.at[step, sub], other.at[step, sub],
            sib_send.at[step, sub], sib_recv.at[step, sub], blk, sib,
        )

    gain = gain_ref[...]
    wide = tok.shape[2]
    width = 2 * wide
    for sub in range(SUBS):
        here = piece_rows(head, sub)
        loads[sub].wait()
        tok_in[sub].wait_recv()
        left, right = tok[0, here, :], tok[1, here, :]
        mean_row = (
            jnp.sum(left, axis=-1, keepdims=True) + jnp.sum(right, axis=-1, keepdims=True)
        ) / width
        left = left - mean_row
        right = right - mean_row
        spread = (
            jnp.sum(left * left, axis=-1, keepdims=True)
            + jnp.sum(right * right, axis=-1, keepdims=True)
        ) / width
        scale = lax.rsqrt(spread + 1e-06)
        ring[0, sub, :, :wide] = (left * scale * gain[:, :wide]).astype(BF16)
        ring[0, sub, :, wide:] = (right * scale * gain[:, wide:]).astype(BF16)
        ring_copy(0, sub).start()
    for sub in range(SUBS):
        normed[piece_rows(head, sub), :] = ring[0, sub]

    def keys_of(chunk):
        kbuf[: chunk.shape[0], :] = dot(chunk, qkv[1]).astype(BF16)

    def values_of(chunk):
        vbuf[:, : chunk.shape[0]] = dot(chunk, qkv[2]).astype(BF16).T

    def attend(which, keys):
        scores = []
        for pair in which:
            base = pair * per_pair // quad * quad
            scores.append(dot(kbuf[:keys, base : base + quad], qbd[pair]))
        for pair, score in zip(which, scores):
            before = peak[pair]
            now = jnp.maximum(before, jnp.max(score, axis=0, keepdims=True))
            weights = jnp.exp(score - now)
            factor = jnp.exp(before - now)
            peak[pair] = now
            total[pair] = total[pair] * factor + jnp.sum(weights, axis=0, keepdims=True)
            mixed = dot(
                vbuf[pair * per_pair : (pair + 1) * per_pair, :keys], weights.astype(BF16)
            )
            acc[pair] = acc[pair] * factor + mixed

    def own_chunk():
        return ring[0].reshape(rows, width)

    def two_chunks(step):
        return jnp.concatenate(
            [ring[step].reshape(rows, width), other[step].reshape(rows, width)], axis=0
        )

    def part_chunk(step, first):
        subs = slice(first, first + SUBS // 2)
        return jnp.concatenate(
            [ring[step, subs].reshape(half, width), other[step, subs].reshape(half, width)], axis=0
        )

    def arrive(step, sub):
        ring_copy(step - 1, sub).wait_recv()
        if sub < SUBS // 2:
            @pl.when(step < last)
            def _():
                ring_copy(step, sub).start()
        else:
            @pl.when(step < last - 1)
            def _():
                ring_copy(step, sub).start()
        sib_copy(step, sub).start()

    def met(step, first, past):
        for sub in range(first, past):
            sib_copy(step, sub).wait_recv()

    low, high = range(pairs // 2), range(pairs // 2, pairs)

    def hop(step, chunk_of, keys):
        arrive(step, 0)
        keys_of(chunk_of())
        arrive(step, 1)
        values_of(chunk_of())
        arrive(step, 2)
        attend(low, keys)
        arrive(step, 3)
        attend(high, keys)

    weights_in[1].wait()
    keys_of(own_chunk())
    arrive(1, 0)
    weights_in[2].wait()
    values_of(own_chunk())
    arrive(1, 1)
    weights_in[0].wait()
    queries = (dot(normed[...], qkv[0]) * (HEAD_DIM ** -0.5)).astype(BF16)
    per_pair = 2 * HEAD_DIM
    quad = qbd.shape[1]
    lane = lax.broadcasted_iota(jnp.int32, (rows, quad), 1)
    for pair in range(pairs):
        base = pair * per_pair // quad * quad
        block = queries[:, base : base + quad]
        both = []
        for inner in range(2):
            first = pair * per_pair + inner * HEAD_DIM - base
            keep = (lane >= first) & (lane < first + HEAD_DIM)
            both.append(jnp.where(keep, block, jnp.zeros_like(block)))
        qbd[pair] = jnp.concatenate(both, axis=0).T
    arrive(1, 2)
    attend(low, rows)
    arrive(1, 3)
    attend(high, rows)

    def ring_step(step, carry):
        met(step - 1, 0, SUBS)
        hop(step, lambda: two_chunks(step - 1), 2 * rows)
        return carry

    lax.fori_loop(2, last, ring_step, 0)
    mid = SUBS // 2
    met(last - 1, 0, mid)
    keys_of(part_chunk(last - 1, 0))
    values_of(part_chunk(last - 1, 0))
    attend(range(pairs), rows)
    arrive(last, 0)
    met(last - 1, mid, SUBS)
    keys_of(part_chunk(last - 1, mid))
    values_of(part_chunk(last - 1, mid))
    arrive(last, 1)
    attend(range(pairs), rows)
    met(last, 0, mid)
    keys_of(part_chunk(last, 0))
    values_of(part_chunk(last, 0))
    attend(range(pairs), rows)

    pair_lane = lax.broadcasted_iota(jnp.int32, (rows, per_pair), 1)
    for pair in range(pairs):
        done = (acc[pair] * (1.0 / total[pair])).astype(BF16).T
        att[:, pair * per_pair : (pair + 1) * per_pair] = jnp.where(
            pair_lane < HEAD_DIM, done[:rows], done[rows:]
        )

    weights_in[3].wait()

    def tile_rows(ref, side):
        return jnp.concatenate(
            [
                ref[pl.ds(pl.multiple_of(side * cols + row * GW, 16), cols), :]
                for row in range(ROWS_DEV)
            ],
            axis=0,
        )

    part_send[...] = dot(tile_rows(att, sib), out_w[...]).astype(BF16)
    part_copy = remote(part_send, part_recv, part_sem.at[0], part_sem.at[1], blk, sib)
    part_copy.start()
    own = dot(tile_rows(att, head), out_w[...])
    residual = jnp.concatenate([tile_rows(tok.at[0], head), tile_rows(tok.at[1], head)], axis=1)
    own = own + residual
    weights_in[4].wait()
    weights_in[5].wait()
    part_copy.wait()
    block_out = (own + part_recv[...].astype(F32)).astype(BF16)

    cells = ROWS_DEV * cols
    fine_in = layer_norm(dot(block_out, lat_w[0]), gains_ref[0, 0:1]).astype(BF16).astype(F32)
    for row in range(ROWS_DEV):
        fpad[1 + row, 8 : 8 + cols, :] = fine_in[row * cols : (row + 1) * cols]

    def halo(pad, first_row, last_row, inner, index):
        below = last_row + 1
        src_col = pl.multiple_of(inner - (inner - 8) * head, 8)
        dst_col = pl.multiple_of((8 + inner) * head, 8)
        tile = pl.ds(src_col, 8)
        into = pl.ds(dst_col, 8)
        body_cols = pl.ds(8, inner)

        def make(src, dst, place, to_blk, to_head):
            return remote(
                src, dst, halo_send.at[index + place], halo_recv.at[index + place], to_blk, to_head
            )

        span = pl.ds(first_row, last_row - first_row + 1)
        return [
            (None, make(pad.at[span, tile], pad.at[span, into], 0, blk, sib)),
            ("up", make(pad.at[first_row, body_cols], pad.at[below, body_cols], 1, blk - 1, head)),
            ("up", make(pad.at[first_row, tile], pad.at[below, into], 2, blk - 1, sib)),
            ("down", make(pad.at[last_row, body_cols], pad.at[0, body_cols], 3, blk + 1, head)),
            ("down", make(pad.at[last_row, tile], pad.at[0, into], 4, blk + 1, sib)),
        ]

    def guarded(way, action):
        if way is None:
            action()
        else:
            pl.when(has_up if way == "up" else has_down)(action)

    opposite = {None: None, "up": "down", "down": "up"}
    fine_halo = halo(fpad, 1, ROWS_DEV, cols, 0)
    for way, copy in fine_halo:
        guarded(way, copy.start)

    tall = block_out[:cols]
    for row in range(1, ROWS_DEV):
        tall = jnp.maximum(tall, block_out[row * cols : (row + 1) * cols])
    pool_rows = ccol.shape[0]
    at_row = lax.broadcasted_iota(jnp.int32, (pool_rows, cols), 0)
    at_col = lax.broadcasted_iota(jnp.int32, (pool_rows, cols), 1)
    pooled = jnp.maximum(
        dot((at_col == 2 * at_row).astype(F32).astype(BF16), tall),
        dot((at_col == 2 * at_row + 1).astype(F32).astype(BF16), tall),
    ).astype(BF16)
    coarse_cols = cols // 2
    coarse_in = layer_norm(dot(pooled, lat_w[1]), gains_ref[1, 0:1]).astype(BF16).astype(F32)
    cpad[1, 8 : 8 + coarse_cols, :] = coarse_in[:coarse_cols]
    coarse_halo = halo(cpad, 1, 1, coarse_cols, 5)
    for way, copy in coarse_halo:
        guarded(way, copy.start)

    channels = fine_ref.shape[-1]
    for way, copy in fine_halo:
        guarded(opposite[way], copy.wait_recv)
    for a in range(3):
        for b in range(3):
            place = (3 * a + b) * channels
            for row in range(ROWS_DEV):
                fcol[row * cols : (row + 1) * cols, place : place + channels] = fpad[
                    row + a, 7 + b : 7 + b + cols, :
                ].astype(BF16)
    fine_out = layer_norm(dot(fcol[...], conv_w[0]), gains_ref[0, 1:2]).astype(BF16)
    for row in range(ROWS_DEV):
        fine_ref[row] = fine_out[row * cols : (row + 1) * cols]

    for way, copy in coarse_halo:
        guarded(opposite[way], copy.wait_recv)
    for a in range(3):
        for b in range(3):
            place = (3 * a + b) * channels
            ccol[:, place : place + channels] = cpad[a, 7 + b : 7 + b + pool_rows, :].astype(BF16)
    coarse_out = layer_norm(dot(ccol[...], conv_w[1]), gains_ref[1, 1:2]).astype(BF16)
    coarse_ref[0] = coarse_out[:coarse_cols]

    for way, copy in fine_halo + coarse_halo:
        guarded(way, copy.wait_send)
    for sub in range(SUBS):
        tok_out[sub].wait_send()
        ring_copy(0, sub).wait_send()

    def drain(step, carry):
        for sub in range(SUBS):
            sib_copy(step, sub).wait_send()
            if sub < SUBS // 2:
                ring_copy(step, sub).wait_send()
            else:
                @pl.when(step < last - 1)
                def _():
                    ring_copy(step, sub).wait_send()

        return carry

    lax.fori_loop(1, last, drain, 0)
    for sub in range(SUBS // 2):
        sib_copy(last, sub).wait_send()


def body(tokens, norm_gain, qkv_weight, out_weight, lateral_weight, conv_weight, level_gains):
    count = lax.axis_size("blk")
    rows, wide = tokens.shape
    width = qkv_weight.shape[1]
    heads_width = qkv_weight.shape[2]
    channels = lateral_weight.shape[2]
    per_pair = 2 * HEAD_DIM
    pairs = heads_width // per_pair
    quad = 2 * per_pair
    hops = count // 2 + 1
    cols = GW // 2
    cells = ROWS_DEV * cols
    coarse_cols = cols // 2
    pool_rows = -(-coarse_cols // 16) * 16
    conv_depth = 9 * channels
    vmem = pl.BlockSpec(memory_space=pltpu.VMEM)
    hbm = pl.BlockSpec(memory_space=pl.ANY)
    dma = pltpu.SemaphoreType.DMA
    return pl.pallas_call(
        functools.partial(kernel, count),
        out_shape=(
            jax.ShapeDtypeStruct((ROWS_DEV, cols, channels), BF16),
            jax.ShapeDtypeStruct((ROWS_DEV // 2, coarse_cols, channels), BF16),
        ),
        in_specs=[hbm, vmem, hbm, hbm, hbm, hbm, vmem],
        out_specs=(vmem, vmem),
        scratch_shapes=[
            pltpu.VMEM((2, rows, wide), F32),
            pltpu.VMEM(qkv_weight.shape, BF16),
            pltpu.VMEM(out_weight.shape, BF16),
            pltpu.VMEM(lateral_weight.shape, BF16),
            pltpu.VMEM((2, conv_depth, channels), BF16),
            pltpu.VMEM((rows, width), BF16),
            pltpu.VMEM((hops, SUBS, rows // SUBS, width), BF16),
            pltpu.VMEM((hops, SUBS, rows // SUBS, width), BF16),
            pltpu.VMEM((pairs, quad, 2 * rows), BF16),
            pltpu.VMEM((2 * rows, heads_width), BF16),
            pltpu.VMEM((heads_width, 2 * rows), BF16),
            pltpu.VMEM((pairs, per_pair, 2 * rows), F32),
            pltpu.VMEM((pairs, 1, 2 * rows), F32),
            pltpu.VMEM((pairs, 1, 2 * rows), F32),
            pltpu.VMEM((rows, heads_width), BF16),
            pltpu.VMEM((cells, width), BF16),
            pltpu.VMEM((cells, width), BF16),
            pltpu.VMEM((ROWS_DEV + 2, cols + 16, channels), F32),
            pltpu.VMEM((3, pool_rows + 16, channels), F32),
            pltpu.VMEM((cells, conv_depth), BF16),
            pltpu.VMEM((pool_rows, conv_depth), BF16),
            dma((6 + SUBS,)),
            dma((SUBS,)),
            dma((SUBS,)),
            dma((hops, SUBS)),
            dma((hops, SUBS)),
            dma((hops, SUBS)),
            dma((hops, SUBS)),
            dma((2,)),
            dma((10,)),
            dma((10,)),
        ],
        compiler_params=pltpu.CompilerParams(
            collective_id=0, has_side_effects=True, vmem_limit_bytes=54912 * 1024
        ),
    )(
        tokens,
        norm_gain.reshape(1, width),
        qkv_weight,
        out_weight,
        lateral_weight,
        conv_weight.reshape(2, conv_depth, channels),
        level_gains,
    )


def solution(mesh):
    in_specs = (
        P(("groups", "blk"), "head"),
        P(),
        P(None, None, "head"),
        P("head", None),
        P(),
        P(),
        P(),
    )
    out_specs = (P(("groups", "blk"), "head", None), P(("groups", "blk"), "head", None))
    return jax.shard_map(body, mesh=mesh, in_specs=in_specs, out_specs=out_specs, check_vma=False)
```
